32 devices in a mesh: pts: 16 (over z, y, x), ctr: 2 (over core).
Axes of the slice: x: 2, y: 2, z: 4, core: 2. Of those that a mesh axis runs over, the one named last changes fastest.
Arguments:
- points: bfloat16 [32, 32768], P(None, 'pts'), may hold values from -6 to 6
- centres: bfloat16 [32, 16384], P(None, 'ctr'), may hold values from -6 to 6
- coef: float32 [16, 16384], P(None, 'ctr'), may hold values from -6 to 6
- resid: float32 [16, 16384], P(None, 'ctr'), may hold values from -6 to 6
- direction: float32 [16, 16384], P(None, 'ctr'), may hold values from -6 to 6
- precond: float32 [16384], P('ctr'), may hold values from 0.5 to 4
Outputs:
- coef_next: float32 [16, 16384], P(None, 'ctr')
- resid_next: float32 [16, 16384], P(None, 'ctr')
- dir_next: float32 [16, 16384], P(None, 'ctr')
The draws below stay inside these ranges and needn't reach their ends.
All inputs are finite; a program needn't handle non-finite values.
Results may differ from the reference program's by a relative error of at most 0.0012.
Values may be sent and summed in bfloat16 or wider, within the bound.
No kernel may reach another device: no remote copies, remote signals or barrier semaphores. Data moves between devices by JAX's collectives and lax.ppermute only.
A program may use at most 128 MiB of HBM per device.

```python
import math
import jax
import jax.numpy as jnp
from jax import lax

FEAT = 32
CTR_DEV = 8192
P_DEV = 2048
TARGETS = 16
CENTRES = 16384
NPTS = 32768
N_PTS = 16
N_CTR = 2


def block_scale(rng, shape, shards, low, high):
    def one(axis_at, shards_of):
        steps = jax.random.uniform(jax.random.fold_in(jax.random.fold_in(rng, 6), axis_at), (shards_of,), jnp.float32, low / len(shards), high / len(shards))
        return jnp.repeat(jnp.exp(steps), shape[axis_at] // shards_of).reshape((-1,) + (1,) * (len(shape) - axis_at - 1))

    gain = one(*shards[0])
    for cut in shards[1:]:
        gain = gain * one(*cut)
    return gain


def centred(key, dims, width, most, cuts=(), held_as=jnp.bfloat16):
    values = width * jax.random.normal(key, dims, jnp.float32)
    if cuts:
        values = values * block_scale(key, dims, cuts, -0.22, 0.18)
    return jnp.clip(values, -most, most).astype(held_as)


def setup_inputs(seed: int = 0) -> dict:
    seeds = jax.random.split(jax.random.key(seed), 7)
    points = centred(seeds[0], (FEAT, NPTS), 1.0, 6.0, ((1, 16),))
    centres = centred(seeds[1], (FEAT, CENTRES), 1.0, 6.0, ((1, 2),))
    coef = centred(seeds[2], (TARGETS, CENTRES), 1.0, 6.0, ((1, 2),), jnp.float32)
    resid = centred(seeds[3], (TARGETS, CENTRES), 1.0, 6.0, ((1, 2),), jnp.float32)
    direction = centred(seeds[4], (TARGETS, CENTRES), 1.0, 6.0, ((1, 2),), jnp.float32)
    precond = jnp.clip(jnp.exp(math.log(4.0) - 2.0794415 * jax.random.uniform(seeds[5], (CENTRES,), jnp.float32) ** block_scale(seeds[5], (CENTRES,), ((0, 2),), -0.2, 0.2)), 0.5, 4.0)
    return dict(points=points, centres=centres, coef=coef, resid=resid, direction=direction, precond=precond)


def reference(points, centres, coef, resid, direction, precond):
    cent32 = centres.astype(jnp.float32)
    csq = jnp.sum(cent32 * cent32, axis=0)
    dirb = direction.astype(jnp.bfloat16)
    blocks = points.reshape(FEAT, N_PTS, P_DEV).transpose(1, 0, 2)

    def step(acc, block):
        pts32 = block.astype(jnp.float32)
        xsq = jnp.sum(pts32 * pts32, axis=0)
        cross = lax.dot_general(block, centres, (((0,), (0,)), ((), ())), preferred_element_type=jnp.float32)
        kern = jnp.exp(-0.125 * (xsq[:, None] + csq[None, :] - 2.0 * cross)).astype(jnp.bfloat16)
        fitted = jnp.zeros((TARGETS, P_DEV), jnp.float32)
        for group in range(N_CTR):
            low = group * CTR_DEV
            part = lax.dot_general(dirb[:, low:low + CTR_DEV], kern[:, low:low + CTR_DEV], (((1,), (1,)), ((), ())), preferred_element_type=jnp.float32)
            part = lax.optimization_barrier(part.astype(jnp.bfloat16))
            fitted = fitted + part.astype(jnp.float32)
        acc = acc + jnp.dot(fitted.astype(jnp.bfloat16), kern, preferred_element_type=jnp.float32)
        return acc, None

    colsum, _ = lax.scan(step, jnp.zeros((TARGETS, CENTRES), jnp.float32), blocks)
    rz = jnp.sum(resid * resid * precond[None, :], axis=1)
    image = colsum * (2048.0 / NPTS) + 0.5 * direction
    alpha = rz / jnp.sum(direction * image, axis=1)
    coef_next = coef + alpha[:, None] * direction
    resid_next = resid - alpha[:, None] * image
    scaled = precond[None, :] * resid_next
    rz_new = jnp.sum(resid_next * scaled, axis=1)
    dir_next = scaled + (rz_new / rz)[:, None] * direction
    return coef_next, resid_next, dir_next
```

```python
import functools
import math

import jax
import jax.numpy as jnp
from jax import lax
from jax.experimental import pallas as pl
from jax.experimental.pallas import tpu as pltpu
from jax.sharding import PartitionSpec as P

MIB = 2**20
F32 = jnp.float32
BF16 = jnp.bfloat16
RATE = 0.25 * math.log2(math.e)
DEPTH = 128
VMEM = pl.BlockSpec(memory_space=pltpu.VMEM)


def tile_of(index, size):
    return pl.ds(pl.multiple_of(index * size, size), size)


def split3(value):
    first = value.astype(BF16).astype(F32)
    rest = value - first
    second = rest.astype(BF16).astype(F32)
    return first, second, rest - second


def rows_of(rows, block):
    at = lax.broadcasted_iota(jnp.int32, block, 0)
    out = jnp.zeros(block, F32)
    for i, row in enumerate(rows):
        out = jnp.where(at == i, row, out)
    return out


def fit_kernel(parts, width, pts_ref, cen_ref, dir_ref, *refs):
    kern, (fit_ref, xa_ref, ca_ref, db_ref) = refs[:parts], refs[parts:]
    feat, num = pts_ref.shape
    ctr = cen_ref.shape[1]
    pts = pts_ref[...].astype(F32)
    terms = list(split3(pts * RATE))
    norm = split3(jnp.sum(pts * pts, axis=0, keepdims=True) * (-0.5 * RATE))
    terms.append(rows_of(list(norm) + [1.0, 1.0, 1.0], (DEPTH - 3 * feat, num)))
    xa_ref[...] = jnp.concatenate(terms, axis=0).T.astype(BF16)
    cen = cen_ref[...]
    for i in range(3):
        ca_ref[i * feat : (i + 1) * feat, :] = cen
    cen = cen.astype(F32)
    norm = split3(jnp.sum(cen * cen, axis=0, keepdims=True) * (-0.5 * RATE))
    ca_ref[3 * feat :, :] = rows_of([1.0, 1.0, 1.0] + list(norm), (DEPTH - 3 * feat, ctr)).astype(BF16)
    db_ref[...] = dir_ref[...].astype(BF16)
    rows = num // parts

    def body(j, acc):
        col = tile_of(j, width)
        out = []
        for p in range(parts):
            logk = jnp.dot(xa_ref[p * rows : (p + 1) * rows, :], ca_ref[:, col], preferred_element_type=F32)
            tile = jnp.exp2(logk).astype(BF16)
            kern[p][:, col] = tile
            out.append(lax.dot_general(db_ref[:, col], tile, (((1,), (1,)), ((), ())), preferred_element_type=F32))
        return acc + jnp.concatenate(out, axis=1)

    acc = lax.fori_loop(0, ctr // width, body, jnp.zeros(fit_ref.shape, F32))
    fit_ref[...] = acc.astype(BF16)


def col_kernel(parts, groups, width, *refs):
    fits, kern, (out_ref,) = refs[:groups], refs[groups : groups + parts], refs[groups + parts :]
    fitted = fits[0][...].astype(F32)
    for ref in fits[1:]:
        fitted = fitted + ref[...].astype(F32)
    fitted = fitted.astype(BF16)
    rows = kern[0].shape[0]
    steps = out_ref.shape[2] // width
    for chunk in range(out_ref.shape[0]):

        @pl.loop(0, steps)
        def _(j):
            col = tile_of(chunk * steps + j, width)
            acc = None
            for p in range(parts):
                term = jnp.dot(fitted[:, p * rows : (p + 1) * rows], kern[p][:, col], preferred_element_type=F32)
                acc = term if acc is None else acc + term
            out_ref[chunk, :, tile_of(j, width)] = acc


def width_of(size, most):
    width = most
    while size % width:
        width //= 2
    return width


def fit_parts(points, centres, direction, parts):
    num, ctr = points.shape[1], centres.shape[1]
    targets = direction.shape[0]
    out = pl.pallas_call(
        functools.partial(fit_kernel, parts, width_of(ctr, 1024)),
        out_shape=[jax.ShapeDtypeStruct((num // parts, ctr), BF16)] * parts + [jax.ShapeDtypeStruct((targets, num), BF16)],
        in_specs=[VMEM] * 3,
        out_specs=[VMEM] * (parts + 1),
        scratch_shapes=[pltpu.VMEM((num, DEPTH), BF16), pltpu.VMEM((DEPTH, ctr), BF16), pltpu.VMEM((targets, ctr), BF16)],
        compiler_params=pltpu.CompilerParams(vmem_limit_bytes=20 * MIB),
    )(points, centres, direction)
    return out[:parts], out[parts]


def col_sums(fits, kern, chunks):
    targets = fits[0].shape[0]
    ctr = kern[0].shape[1]
    size = ctr // chunks
    return pl.pallas_call(
        functools.partial(col_kernel, len(kern), len(fits), width_of(size, 1024)),
        out_shape=jax.ShapeDtypeStruct((chunks, targets, size), F32),
        in_specs=[VMEM] * (len(fits) + len(kern)),
        out_specs=VMEM,
        compiler_params=pltpu.CompilerParams(vmem_limit_bytes=8 * MIB),
    )(*fits, *kern)


def radices(size):
    out, prime = [], 2
    while size > 1:
        while size % prime == 0:
            out.append(prime)
            size //= prime
        prime += 1
    return out


def sum_over_pts(chunks):
    num_pts, num_ctr = lax.axis_size("pts"), lax.axis_size("ctr")
    me, odd = lax.axis_index("pts"), lax.axis_index("ctr") % 2

    def send(value, partner):
        pairs = [
            (p * num_ctr + c, partner(p, c % 2) * num_ctr + c) for p in range(num_pts) for c in range(num_ctr)
        ]
        return lax.ppermute(value, ("pts", "ctr"), pairs)

    def bit(phase, odd):
        return 1 + (odd ^ phase)

    digit = [(me // (1 + (odd ^ phase))) % 2 for phase in range(2)]
    value = chunks
    for phase in range(2):
        half = value.reshape((2, value.shape[0] // 2) + value.shape[1:])
        keep = lax.dynamic_index_in_dim(half, digit[phase], 0, False)
        give = lax.dynamic_index_in_dim(half, 1 - digit[phase], 0, False)
        value = keep + send(give, lambda p, c: p ^ bit(phase, c))
    stride = 4
    for radix in radices(num_pts // 4):
        mine = (me // stride) % radix
        got = [value]
        for k in range(1, radix):

            def partner(p, c):
                d = (p // stride) % radix
                return p + ((d + k) % radix - d) * stride

            got.append(send(value, partner))
        if radix == 2:
            value = got[0] + got[1]
        else:
            stack = jnp.stack(got)
            value = sum(lax.dynamic_index_in_dim(stack, (mine - d) % radix, 0, False) for d in range(radix))
        stride *= radix
    for phase in (1, 0):
        other = send(value, lambda p, c: p ^ bit(phase, c))
        pair = (jnp.concatenate([value, other]), jnp.concatenate([other, value]))
        value = jnp.where(digit[phase] == 0, pair[0], pair[1])
    return value


def shards(points, centres, coef, resid, direction, precond):
    num_pts, num_ctr = lax.axis_size("pts"), lax.axis_size("ctr")
    num, ctr = points.shape[1], centres.shape[1]
    parts = 4
    kern, part = fit_parts(points, centres, direction, parts)
    fits = [part]
    for k in range(1, num_ctr):
        fits.append(lax.ppermute(part, "ctr", [(c, (c + k) % num_ctr) for c in range(num_ctr)]))
    if num_ctr > 2:
        stack = jnp.stack(fits)
        fits = [
            lax.dynamic_index_in_dim(stack, (lax.axis_index("ctr") - c) % num_ctr, 0, False) for c in range(num_ctr)
        ]
    chunks = 4
    colsum = sum_over_pts(col_sums(fits, kern, chunks))
    colsum = colsum.transpose(1, 0, 2).reshape(direction.shape)
    scale = 2048.0 / (num * num_pts)
    image = colsum * scale + 0.5 * direction
    rz_part = jnp.sum(resid * resid * precond[None, :], axis=1)
    curv, rz = lax.psum((jnp.sum(direction * image, axis=1), rz_part), "ctr")
    alpha = rz / curv
    coef_next = coef + alpha[:, None] * direction
    resid_next = resid - alpha[:, None] * image
    scaled = precond[None, :] * resid_next
    rz_new = lax.psum(jnp.sum(resid_next * scaled, axis=1), "ctr")
    dir_next = scaled + (rz_new / rz)[:, None] * direction
    return (coef_next, resid_next, dir_next)


def solution(mesh):
    return jax.shard_map(
        shards,
        mesh=mesh,
        in_specs=(
            P(None, "pts"),
            P(None, "ctr"),
            P(None, "ctr"),
            P(None, "ctr"),
            P(None, "ctr"),
            P("ctr"),
        ),
        out_specs=(P(None, "ctr"), P(None, "ctr"), P(None, "ctr")),
        check_vma=False,
    )
```

```python
import functools
import math

import jax
import jax.numpy as jnp
from jax import lax
from jax.experimental import pallas as pl
from jax.experimental.pallas import tpu as pltpu
from jax.sharding import PartitionSpec as P

MIB = 2**20
F32 = jnp.float32
BF16 = jnp.bfloat16
RATE = 0.25 * math.log2(math.e)
DEPTH = 128
VMEM = pl.BlockSpec(memory_space=pltpu.VMEM)


def tile_of(index, size):
    return pl.ds(pl.multiple_of(index * size, size), size)


def split3(value):
    first = value.astype(BF16).astype(F32)
    rest = value - first
    second = rest.astype(BF16).astype(F32)
    return first, second, rest - second


def rows_of(rows, block):
    at = lax.broadcasted_iota(jnp.int32, block, 0)
    out = jnp.zeros(block, F32)
    for i, row in enumerate(rows):
        out = jnp.where(at == i, row, out)
    return out


def fit_kernel(parts, width, pts_ref, cen_ref, dir_ref, *refs):
    kern, (fit_ref, xa_ref, ca_ref, db_ref) = refs[:parts], refs[parts:]
    feat, num = pts_ref.shape
    ctr = cen_ref.shape[1]
    pts = pts_ref[...].astype(F32)
    terms = list(split3(pts * RATE))
    norm = split3(jnp.sum(pts * pts, axis=0, keepdims=True) * (-0.5 * RATE))
    terms.append(rows_of(list(norm) + [1.0, 1.0, 1.0], (DEPTH - 3 * feat, num)))
    xa_ref[...] = jnp.concatenate(terms, axis=0).T.astype(BF16)
    cen = cen_ref[...]
    for i in range(3):
        ca_ref[i * feat : (i + 1) * feat, :] = cen
    cen = cen.astype(F32)
    norm = split3(jnp.sum(cen * cen, axis=0, keepdims=True) * (-0.5 * RATE))
    ca_ref[3 * feat :, :] = rows_of([1.0, 1.0, 1.0] + list(norm), (DEPTH - 3 * feat, ctr)).astype(BF16)
    db_ref[...] = dir_ref[...].astype(BF16)
    rows = num // parts

    def body(j, acc):
        col = tile_of(j, width)
        out = []
        for p in range(parts):
            logk = jnp.dot(xa_ref[p * rows : (p + 1) * rows, :], ca_ref[:, col], preferred_element_type=F32)
            tile = jnp.exp2(logk).astype(BF16)
            kern[p][:, col] = tile
            out.append(lax.dot_general(db_ref[:, col], tile, (((1,), (1,)), ((), ())), preferred_element_type=F32))
        return acc + jnp.concatenate(out, axis=1)

    acc = lax.fori_loop(0, ctr // width, body, jnp.zeros(fit_ref.shape, F32))
    fit_ref[...] = acc.astype(BF16)


def digits():
    me, odd = lax.axis_index("pts"), lax.axis_index("ctr") % 2
    low, high = me % 2, (me // 2) % 2
    return jnp.where(odd == 0, low, high), jnp.where(odd == 0, high, low)


def chunk_ids():
    a, b = digits()
    return 2 * (1 - a) + (1 - b), 2 * (1 - a) + b, 2 * a + (1 - b), 2 * a + b


def col_kernel(parts, groups, width, which, *refs):
    fits, kern, outs = refs[:groups], refs[groups : groups + parts], refs[groups + parts :]
    fitted = fits[0][...].astype(F32)
    for ref in fits[1:]:
        fitted = fitted + ref[...].astype(F32)
    fitted = fitted.astype(BF16)
    rows = kern[0].shape[0]
    steps = outs[0].shape[1] // width
    ids = chunk_ids()
    for i, out in zip(which, outs):

        @pl.loop(0, steps)
        def _(j):
            col = tile_of(ids[i] * steps + j, width)
            acc = None
            for p in range(parts):
                term = jnp.dot(fitted[:, p * rows : (p + 1) * rows], kern[p][:, col], preferred_element_type=F32)
                acc = term if acc is None else acc + term
            out[:, tile_of(j, width)] = acc


def width_of(size, most):
    width = most
    while size % width:
        width //= 2
    return width


def fit_parts(points, centres, direction, parts):
    num, ctr = points.shape[1], centres.shape[1]
    targets = direction.shape[0]
    out = pl.pallas_call(
        functools.partial(fit_kernel, parts, width_of(ctr, 1024)),
        out_shape=[jax.ShapeDtypeStruct((num // parts, ctr), BF16)] * parts + [jax.ShapeDtypeStruct((targets, num), BF16)],
        in_specs=[VMEM] * 3,
        out_specs=[VMEM] * (parts + 1),
        scratch_shapes=[pltpu.VMEM((num, DEPTH), BF16), pltpu.VMEM((DEPTH, ctr), BF16), pltpu.VMEM((targets, ctr), BF16)],
        compiler_params=pltpu.CompilerParams(vmem_limit_bytes=8 * MIB),
    )(points, centres, direction)
    return out[:parts], out[parts]


def col_sums(fits, kern, which):
    targets = fits[0].shape[0]
    size = kern[0].shape[1] // 4
    return pl.pallas_call(
        functools.partial(col_kernel, len(kern), len(fits), width_of(size, 1024), which),
        out_shape=[jax.ShapeDtypeStruct((targets, size), F32)] * len(which),
        in_specs=[VMEM] * (len(fits) + len(kern)),
        out_specs=[VMEM] * len(which),
        compiler_params=pltpu.CompilerParams(vmem_limit_bytes=4 * MIB),
    )(*fits, *kern)


def radices(size):
    out, prime = [], 2
    while size > 1:
        while size % prime == 0:
            out.append(prime)
            size //= prime
        prime += 1
    return out


def send_pts(value, partner):
    num_pts, num_ctr = lax.axis_size("pts"), lax.axis_size("ctr")
    pairs = [(p * num_ctr + c, partner(p, c % 2) * num_ctr + c) for p in range(num_pts) for c in range(num_ctr)]
    return lax.ppermute(value, ("pts", "ctr"), pairs)


def along(phase):
    return lambda p, odd: p ^ (1 + (odd ^ phase))


def sum_over_rest(value):
    me, stride = lax.axis_index("pts"), 4
    for radix in radices(lax.axis_size("pts") // 4):
        got = [value]
        for k in range(1, radix):

            def partner(p, odd):
                d = (p // stride) % radix
                return p + ((d + k) % radix - d) * stride

            got.append(send_pts(value, partner))
        if radix == 2:
            value = got[0] + got[1]
        else:
            mine, stack = (me // stride) % radix, jnp.stack(got)
            value = sum(lax.dynamic_index_in_dim(stack, (mine - d) % radix, 0, False) for d in range(radix))
        stride *= radix
    return value


def over_ctr(value):
    num_ctr = lax.axis_size("ctr")
    return [value] + [
        lax.ppermute(value, "ctr", [(c, (c + k) % num_ctr) for c in range(num_ctr)]) for k in range(1, num_ctr)
    ]


def total(refs):
    value = refs[0][...]
    for ref in refs[1:]:
        value = value + ref[...]
    return value[:, :1]


def image_kernel(scale, *refs):
    chunks, (dir_ref, res_ref, pre_ref, image_ref, curv_ref, rz_ref) = refs[:4], refs[4:]
    size = chunks[0].shape[1]
    curv = jnp.zeros(curv_ref.shape, F32)
    for chunk, i in zip(chunks, chunk_ids()):
        col = tile_of(i, size)
        direction = dir_ref[:, col]
        image = chunk[...] * scale + 0.5 * direction
        image_ref[:, col] = image
        curv = curv + jnp.sum(direction * image, axis=1, keepdims=True)
    curv_ref[...] = curv
    resid = res_ref[...]
    rz_ref[...] = jnp.zeros(rz_ref.shape, F32) + jnp.sum(resid * resid * pre_ref[...], axis=1, keepdims=True)


def step_kernel(groups, *refs):
    curvs, rzs = refs[:groups], refs[groups : 2 * groups]
    image_ref, dir_ref, res_ref, pre_ref, coef_ref, coef_out, res_out, new_ref = refs[2 * groups :]
    alpha = total(rzs) / total(curvs)
    coef_out[...] = coef_ref[...] + alpha * dir_ref[...]
    resid = res_ref[...] - alpha * image_ref[...]
    res_out[...] = resid
    new_ref[...] = jnp.zeros(new_ref.shape, F32) + jnp.sum(resid * (pre_ref[...] * resid), axis=1, keepdims=True)


def turn_kernel(groups, *refs):
    news, rzs = refs[:groups], refs[groups : 2 * groups]
    res_ref, pre_ref, dir_ref, out_ref = refs[2 * groups :]
    out_ref[...] = pre_ref[...] * res_ref[...] + (total(news) / total(rzs)) * dir_ref[...]


def small_call(kernel, outs, *args):
    return pl.pallas_call(
        kernel,
        out_shape=[jax.ShapeDtypeStruct(shape, F32) for shape in outs],
        in_specs=[VMEM] * len(args),
        out_specs=[VMEM] * len(outs),
        compiler_params=pltpu.CompilerParams(vmem_limit_bytes=8 * MIB),
    )(*args)


def shards(points, centres, coef, resid, direction, precond):
    num_pts, num_ctr = lax.axis_size("pts"), lax.axis_size("ctr")
    num, full = points.shape[1], direction.shape
    kern, part = fit_parts(points, centres, direction, 4)
    fits = over_ctr(part)
    (give_a,) = col_sums(fits, kern, (0,))
    got_a = send_pts(give_a, along(0))
    (give_b,) = col_sums(fits, kern, (1,))
    got_b = send_pts(give_b, along(0))
    keep_a, keep_b = col_sums(fits, kern, (2, 3))
    mine = send_pts(keep_a + got_a, along(1)) + (keep_b + got_b)
    mine = sum_over_rest(mine)
    near = send_pts(mine, along(1))
    far = send_pts(mine, along(0))
    last = send_pts(near, along(0))
    scale = 2048.0 / (num * num_pts)
    short = (full[0], 128)
    pre = precond.reshape(1, full[1])
    image, curv, rz = small_call(
        functools.partial(image_kernel, scale), [full, short, short], last, far, near, mine, direction, resid, pre
    )
    curvs, rzs = over_ctr(curv), over_ctr(rz)
    coef_next, resid_next, new = small_call(
        functools.partial(step_kernel, num_ctr), [full, full, short], *curvs, *rzs, image, direction, resid, pre, coef
    )
    (dir_next,) = small_call(
        functools.partial(turn_kernel, num_ctr), [full], *over_ctr(new), *rzs, resid_next, pre, direction
    )
    return (coef_next, resid_next, dir_next)


def solution(mesh):
    return jax.shard_map(
        shards,
        mesh=mesh,
        in_specs=(
            P(None, "pts"),
            P(None, "ctr"),
            P(None, "ctr"),
            P(None, "ctr"),
            P(None, "ctr"),
            P("ctr"),
        ),
        out_specs=(P(None, "ctr"), P(None, "ctr"), P(None, "ctr")),
        check_vma=False,
    )
```

```python
import functools
import math

import jax
import jax.numpy as jnp
from jax import lax
from jax.experimental import pallas as pl
from jax.experimental.pallas import tpu as pltpu
from jax.sharding import PartitionSpec as P

MIB = 2**20
F32 = jnp.float32
BF16 = jnp.bfloat16
RATE = 0.25 * math.log2(math.e)
DEPTH = 128
VMEM = pl.BlockSpec(memory_space=pltpu.VMEM)


def tile_of(index, size):
    return pl.ds(pl.multiple_of(index * size, size), size)


def split3(value):
    first = value.astype(BF16).astype(F32)
    rest = value - first
    second = rest.astype(BF16).astype(F32)
    return first, second, rest - second


def rows_of(rows, block):
    at = lax.broadcasted_iota(jnp.int32, block, 0)
    out = jnp.zeros(block, F32)
    for i, row in enumerate(rows):
        out = jnp.where(at == i, row, out)
    return out


def fit_kernel(parts, width, pts_hbm, cen_hbm, dir_hbm, *refs):
    kern, (fit_ref, pts_ref, cen_ref, dir_ref, xa_ref, ca_ref, db_ref, sems) = refs[:parts], refs[parts:]
    pairs = ((pts_hbm, pts_ref), (cen_hbm, cen_ref), (dir_hbm, dir_ref))
    copies = [pltpu.make_async_copy(source, target, sems.at[i]) for i, (source, target) in enumerate(pairs)]
    for copy in copies:
        copy.start()
    feat, num = pts_ref.shape
    ctr = cen_ref.shape[1]
    copies[0].wait()
    pts = pts_ref[...].astype(F32)
    terms = list(split3(pts * RATE))
    norm = split3(jnp.sum(pts * pts, axis=0, keepdims=True) * (-0.5 * RATE))
    terms.append(rows_of(list(norm) + [1.0, 1.0, 1.0], (DEPTH - 3 * feat, num)))
    xa_ref[...] = jnp.concatenate(terms, axis=0).T.astype(BF16)
    copies[1].wait()
    cen = cen_ref[...]
    for i in range(3):
        ca_ref[i * feat : (i + 1) * feat, :] = cen
    cen = cen.astype(F32)
    norm = split3(jnp.sum(cen * cen, axis=0, keepdims=True) * (-0.5 * RATE))
    ca_ref[3 * feat :, :] = rows_of([1.0, 1.0, 1.0] + list(norm), (DEPTH - 3 * feat, ctr)).astype(BF16)
    copies[2].wait()
    db_ref[...] = dir_ref[...].astype(BF16)
    rows = num // parts

    def body(j, acc):
        col = tile_of(j, width)
        out = []
        for p in range(parts):
            logk = jnp.dot(xa_ref[p * rows : (p + 1) * rows, :], ca_ref[:, col], preferred_element_type=F32)
            tile = jnp.exp2(logk).astype(BF16)
            kern[p][:, col] = tile
            out.append(lax.dot_general(db_ref[:, col], tile, (((1,), (1,)), ((), ())), preferred_element_type=F32))
        return acc + jnp.concatenate(out, axis=1)

    acc = lax.fori_loop(0, ctr // width, body, jnp.zeros(fit_ref.shape, F32))
    fit_ref[...] = acc.astype(BF16)


def digits():
    me, odd = lax.axis_index("pts"), lax.axis_index("ctr") % 2
    low, high = me % 2, (me // 2) % 2
    return jnp.where(odd == 0, low, high), jnp.where(odd == 0, high, low)


def chunk_ids():
    a, b = digits()
    return 2 * (1 - a) + (1 - b), 2 * (1 - a) + b, 2 * a + (1 - b), 2 * a + b


def col_kernel(parts, groups, width, which, *refs):
    fits, kern, outs = refs[:groups], refs[groups : groups + parts], refs[groups + parts :]
    fitted = fits[0][...].astype(F32)
    for ref in fits[1:]:
        fitted = fitted + ref[...].astype(F32)
    fitted = fitted.astype(BF16)
    rows = kern[0].shape[0]
    steps = outs[0].shape[1] // width
    ids = chunk_ids()
    for i, out in zip(which, outs):

        @pl.loop(0, steps)
        def _(j):
            col = tile_of(ids[i] * steps + j, width)
            acc = None
            for p in range(parts):
                term = jnp.dot(fitted[:, p * rows : (p + 1) * rows], kern[p][:, col], preferred_element_type=F32)
                acc = term if acc is None else acc + term
            out[:, tile_of(j, width)] = acc


def width_of(size, most):
    width = most
    while size % width:
        width //= 2
    return width


def fit_parts(points, centres, direction, parts):
    num, ctr = points.shape[1], centres.shape[1]
    targets = direction.shape[0]
    out = pl.pallas_call(
        functools.partial(fit_kernel, parts, width_of(ctr, 1024)),
        out_shape=[jax.ShapeDtypeStruct((num // parts, ctr), BF16)] * parts + [jax.ShapeDtypeStruct((targets, num), BF16)],
        in_specs=[pl.BlockSpec(memory_space=pl.ANY)] * 3,
        out_specs=[VMEM] * (parts + 1),
        scratch_shapes=[
            pltpu.VMEM(points.shape, BF16),
            pltpu.VMEM(centres.shape, BF16),
            pltpu.VMEM(direction.shape, F32),
            pltpu.VMEM((num, DEPTH), BF16),
            pltpu.VMEM((DEPTH, ctr), BF16),
            pltpu.VMEM((targets, ctr), BF16),
            pltpu.SemaphoreType.DMA((3,)),
        ],
        compiler_params=pltpu.CompilerParams(vmem_limit_bytes=8 * MIB),
    )(*[pltpu.with_memory_space_constraint(value, pltpu.HBM) for value in (points, centres, direction)])
    return out[:parts], out[parts]


def col_sums(fits, kern, which):
    targets = fits[0].shape[0]
    size = kern[0].shape[1] // 4
    return pl.pallas_call(
        functools.partial(col_kernel, len(kern), len(fits), width_of(size, 1024), which),
        out_shape=[jax.ShapeDtypeStruct((targets, size), F32)] * len(which),
        in_specs=[VMEM] * (len(fits) + len(kern)),
        out_specs=[VMEM] * len(which),
        compiler_params=pltpu.CompilerParams(vmem_limit_bytes=4 * MIB),
    )(*fits, *kern)


def radices(size):
    out, prime = [], 2
    while size > 1:
        while size % prime == 0:
            out.append(prime)
            size //= prime
        prime += 1
    return out


def send_pts(value, partner):
    num_pts, num_ctr = lax.axis_size("pts"), lax.axis_size("ctr")
    pairs = [(p * num_ctr + c, partner(p, c % 2) * num_ctr + c) for p in range(num_pts) for c in range(num_ctr)]
    return lax.ppermute(value, ("pts", "ctr"), pairs)


def along(phase):
    return lambda p, odd: p ^ (1 + (odd ^ phase))


def sum_over_rest(value):
    rest = lax.axis_size("pts") // 4
    twos = rest & -rest
    for k in range(twos.bit_length() - 1):
        mask = 4 * (2 * 2**k - 1)
        value = value + send_pts(value, lambda p, odd: p ^ mask)
    me, stride = lax.axis_index("pts"), 4 * twos
    for radix in radices(rest // twos):
        got = [value]
        for k in range(1, radix):

            def partner(p, odd):
                d = (p // stride) % radix
                return p + ((d + k) % radix - d) * stride

            got.append(send_pts(value, partner))
        mine, stack = (me // stride) % radix, jnp.stack(got)
        value = sum(lax.dynamic_index_in_dim(stack, (mine - d) % radix, 0, False) for d in range(radix))
        stride *= radix
    return value


def over_ctr(value):
    num_ctr = lax.axis_size("ctr")
    return [value] + [
        lax.ppermute(value, "ctr", [(c, (c + k) % num_ctr) for c in range(num_ctr)]) for k in range(1, num_ctr)
    ]


def image_kernel(scale, *refs):
    chunks, (dir_ref, res_ref, pre_ref, image_ref, sums_ref) = refs[:4], refs[4:]
    size = chunks[0].shape[1]
    targets = sums_ref.shape[0] // 4
    sums = [jnp.zeros((targets, 1), F32)] * 4
    for chunk, i in zip(chunks, chunk_ids()):
        col = tile_of(i, size)
        direction, resid, pre = dir_ref[:, col], res_ref[:, col], pre_ref[:, col]
        image = chunk[...] * scale + 0.5 * direction
        image_ref[:, col] = image
        terms = (resid * resid * pre, direction * image, resid * pre * image, image * image * pre)
        sums = [old + jnp.sum(term, axis=1, keepdims=True) for old, term in zip(sums, terms)]
    for i, value in enumerate(sums):
        sums_ref[i * targets : (i + 1) * targets, :] = jnp.broadcast_to(value, (targets, 128))


def step_kernel(groups, *refs):
    image_ref, dir_ref, res_ref, pre_ref, coef_ref, coef_out, res_out, dir_out = refs[groups:]
    targets = dir_ref.shape[0]
    total = refs[0][...]
    for ref in refs[1:groups]:
        total = total + ref[...]
    rz, curv, cross, square = [total[i * targets : (i + 1) * targets, :1] for i in range(4)]
    alpha = rz / curv
    direction = dir_ref[...]
    coef_out[...] = coef_ref[...] + alpha * direction
    resid = res_ref[...] - alpha * image_ref[...]
    res_out[...] = resid
    rz_new = rz - alpha * (2.0 * cross - alpha * square)
    dir_out[...] = pre_ref[...] * resid + (rz_new / rz) * direction


def small_call(kernel, outs, *args):
    return pl.pallas_call(
        kernel,
        out_shape=[jax.ShapeDtypeStruct(shape, F32) for shape in outs],
        in_specs=[VMEM] * len(args),
        out_specs=[VMEM] * len(outs),
        compiler_params=pltpu.CompilerParams(vmem_limit_bytes=8 * MIB),
    )(*args)


def shards(points, centres, coef, resid, direction, precond):
    num_pts, num_ctr = lax.axis_size("pts"), lax.axis_size("ctr")
    num, full = points.shape[1], direction.shape
    kern, part = fit_parts(points, centres, direction, 4)
    fits = over_ctr(part)
    (give_a,) = col_sums(fits, kern, (0,))
    got_a = send_pts(give_a, along(0))
    (give_b,) = col_sums(fits, kern, (1,))
    got_b = send_pts(give_b, along(0))
    keep_a, keep_b = col_sums(fits, kern, (2, 3))
    mine = send_pts(keep_a + got_a, along(1)) + (keep_b + got_b)
    mine = sum_over_rest(mine)
    near = send_pts(mine, along(1))
    far = send_pts(mine, along(0))
    last = send_pts(near, along(0))
    scale = 2048.0 / (num * num_pts)
    pre = precond.reshape(1, full[1])
    image, sums = small_call(
        functools.partial(image_kernel, scale), [full, (4 * full[0], 128)], last, far, near, mine, direction, resid, pre
    )
    return small_call(
        functools.partial(step_kernel, num_ctr), [full] * 3, *over_ctr(sums), image, direction, resid, pre, coef
    )


def solution(mesh):
    return jax.shard_map(
        shards,
        mesh=mesh,
        in_specs=(
            P(None, "pts"),
            P(None, "ctr"),
            P(None, "ctr"),
            P(None, "ctr"),
            P(None, "ctr"),
            P("ctr"),
        ),
        out_specs=(P(None, "ctr"), P(None, "ctr"), P(None, "ctr")),
        check_vma=False,
    )
```

```python
import functools
import math

import jax
import jax.numpy as jnp
from jax import lax
from jax.experimental import pallas as pl
from jax.experimental.pallas import tpu as pltpu
from jax.sharding import PartitionSpec as P

MIB = 2**20
F32 = jnp.float32
BF16 = jnp.bfloat16
RATE = 0.25 * math.log2(math.e)
DEPTH = 128
VMEM = pl.BlockSpec(memory_space=pltpu.VMEM)


def tile_of(index, size):
    return pl.ds(pl.multiple_of(index * size, size), size)


def split3(value):
    first = value.astype(BF16).astype(F32)
    rest = value - first
    second = rest.astype(BF16).astype(F32)
    return first, second, rest - second


def rows_of(rows, block):
    at = lax.broadcasted_iota(jnp.int32, block, 0)
    out = jnp.zeros(block, F32)
    for i, row in enumerate(rows):
        out = jnp.where(at == i, row, out)
    return out


def fit_kernel(parts, width, pts_hbm, cen_hbm, dir_hbm, *refs):
    kern, (fit_ref, pts_ref, cen_ref, dir_ref, xa_ref, ca_ref, db_ref, sems) = refs[:parts], refs[parts:]
    pairs = ((pts_hbm, pts_ref), (cen_hbm, cen_ref), (dir_hbm, dir_ref))
    copies = [pltpu.make_async_copy(source, target, sems.at[i]) for i, (source, target) in enumerate(pairs)]
    for copy in copies:
        copy.start()
    feat, num = pts_ref.shape
    ctr = cen_ref.shape[1]
    copies[0].wait()
    pts = pts_ref[...].astype(F32)
    terms = list(split3(pts * RATE))
    norm = split3(jnp.sum(pts * pts, axis=0, keepdims=True) * (-0.5 * RATE))
    terms.append(rows_of(list(norm) + [1.0, 1.0, 1.0], (DEPTH - 3 * feat, num)))
    xa_ref[...] = jnp.concatenate(terms, axis=0).T.astype(BF16)
    copies[1].wait()
    cen = cen_ref[...]
    for i in range(3):
        ca_ref[i * feat : (i + 1) * feat, :] = cen
    cen = cen.astype(F32)
    norm = split3(jnp.sum(cen * cen, axis=0, keepdims=True) * (-0.5 * RATE))
    ca_ref[3 * feat :, :] = rows_of([1.0, 1.0, 1.0] + list(norm), (DEPTH - 3 * feat, ctr)).astype(BF16)
    copies[2].wait()
    db_ref[...] = dir_ref[...].astype(BF16)
    rows = num // parts

    def body(j, acc):
        col = tile_of(j, width)
        out = []
        for p in range(parts):
            logk = jnp.dot(xa_ref[p * rows : (p + 1) * rows, :], ca_ref[:, col], preferred_element_type=F32)
            tile = jnp.exp2(logk).astype(BF16)
            kern[p][:, col] = tile
            out.append(lax.dot_general(db_ref[:, col], tile, (((1,), (1,)), ((), ())), preferred_element_type=F32))
        return acc + jnp.concatenate(out, axis=1)

    acc = lax.fori_loop(0, ctr // width, body, jnp.zeros(fit_ref.shape, F32))
    fit_ref[...] = acc.astype(BF16)


def digits():
    me, odd = lax.axis_index("pts"), lax.axis_index("ctr") % 2
    low, high = me % 2, (me // 2) % 2
    return jnp.where(odd == 0, low, high), jnp.where(odd == 0, high, low)


def chunk_ids():
    a, b = digits()
    return 2 * (1 - a) + (1 - b), 2 * (1 - a) + b, 2 * a + (1 - b), 2 * a + b


def col_kernel(parts, groups, width, which, *refs):
    fits, kern, outs = refs[:groups], refs[groups : groups + parts], refs[groups + parts :]
    fitted = fits[0][...].astype(F32)
    for ref in fits[1:]:
        fitted = fitted + ref[...].astype(F32)
    fitted = fitted.astype(BF16)
    rows = kern[0].shape[0]
    steps = outs[0].shape[1] // width
    ids = chunk_ids()
    for i, out in zip(which, outs):

        @pl.loop(0, steps)
        def _(j):
            col = tile_of(ids[i] * steps + j, width)
            acc = None
            for p in range(parts):
                term = jnp.dot(fitted[:, p * rows : (p + 1) * rows], kern[p][:, col], preferred_element_type=F32)
                acc = term if acc is None else acc + term
            out[:, tile_of(j, width)] = acc


def width_of(size, most):
    width = most
    while size % width:
        width //= 2
    return width


def fit_parts(points, centres, direction, parts):
    num, ctr = points.shape[1], centres.shape[1]
    targets = direction.shape[0]
    out = pl.pallas_call(
        functools.partial(fit_kernel, parts, width_of(ctr, 1024)),
        out_shape=[jax.ShapeDtypeStruct((num // parts, ctr), BF16)] * parts + [jax.ShapeDtypeStruct((targets, num), BF16)],
        in_specs=[pl.BlockSpec(memory_space=pl.ANY)] * 3,
        out_specs=[VMEM] * (parts + 1),
        scratch_shapes=[
            pltpu.VMEM(points.shape, BF16),
            pltpu.VMEM(centres.shape, BF16),
            pltpu.VMEM(direction.shape, F32),
            pltpu.VMEM((num, DEPTH), BF16),
            pltpu.VMEM((DEPTH, ctr), BF16),
            pltpu.VMEM((targets, ctr), BF16),
            pltpu.SemaphoreType.DMA((3,)),
        ],
        compiler_params=pltpu.CompilerParams(vmem_limit_bytes=8 * MIB),
    )(*[pltpu.with_memory_space_constraint(value, pltpu.HBM) for value in (points, centres, direction)])
    return out[:parts], out[parts]


def col_sums(fits, kern, which):
    targets = fits[0].shape[0]
    size = kern[0].shape[1] // 4
    return pl.pallas_call(
        functools.partial(col_kernel, len(kern), len(fits), width_of(size, 1024), which),
        out_shape=[jax.ShapeDtypeStruct((targets, size), F32)] * len(which),
        in_specs=[VMEM] * (len(fits) + len(kern)),
        out_specs=[VMEM] * len(which),
        compiler_params=pltpu.CompilerParams(vmem_limit_bytes=4 * MIB),
    )(*fits, *kern)


def radices(size):
    out, prime = [], 2
    while size > 1:
        while size % prime == 0:
            out.append(prime)
            size //= prime
        prime += 1
    return out


def send_pts(value, partner):
    num_pts, num_ctr = lax.axis_size("pts"), lax.axis_size("ctr")
    pairs = [(p * num_ctr + c, partner(p, c % 2) * num_ctr + c) for p in range(num_pts) for c in range(num_ctr)]
    return lax.ppermute(value, ("pts", "ctr"), pairs)


def along(phase):
    return lambda p, odd: p ^ (1 + (odd ^ phase))


def sum_over_rest(value):
    rest = lax.axis_size("pts") // 4
    twos = rest & -rest
    for k in range(twos.bit_length() - 1):
        mask = 4 * (2 * 2**k - 1)
        value = value + send_pts(value, lambda p, odd: p ^ mask)
    me, stride = lax.axis_index("pts"), 4 * twos
    for radix in radices(rest // twos):
        got = [value]
        for k in range(1, radix):

            def partner(p, odd):
                d = (p // stride) % radix
                return p + ((d + k) % radix - d) * stride

            got.append(send_pts(value, partner))
        mine, stack = (me // stride) % radix, jnp.stack(got)
        value = sum(lax.dynamic_index_in_dim(stack, (mine - d) % radix, 0, False) for d in range(radix))
        stride *= radix
    return value


def over_ctr(value):
    num_ctr = lax.axis_size("ctr")
    return [value] + [
        lax.ppermute(value, "ctr", [(c, (c + k) % num_ctr) for c in range(num_ctr)]) for k in range(1, num_ctr)
    ]


def image_kernel(scale, *refs):
    chunks, (dir_ref, res_ref, pre_ref, image_ref, sums_ref) = refs[:4], refs[4:]
    size = chunks[0].shape[1]
    targets = sums_ref.shape[0] // 4
    sums = [jnp.zeros((targets, 1), F32)] * 4
    for chunk, i in zip(chunks, chunk_ids()):
        col = tile_of(i, size)
        direction, resid, pre = dir_ref[:, col], res_ref[:, col], pre_ref[:, col]
        image = chunk[...] * scale + 0.5 * direction
        image_ref[:, col] = image
        terms = (resid * resid * pre, direction * image, resid * pre * image, image * image * pre)
        sums = [old + jnp.sum(term, axis=1, keepdims=True) for old, term in zip(sums, terms)]
    for i, value in enumerate(sums):
        sums_ref[i * targets : (i + 1) * targets, :] = jnp.broadcast_to(value, (targets, 128))


def step_kernel(groups, *refs):
    image_ref, dir_ref, res_ref, pre_ref, coef_ref, coef_out, res_out, dir_out = refs[groups:]
    targets = dir_ref.shape[0]
    total = refs[0][...]
    for ref in refs[1:groups]:
        total = total + ref[...]
    rz, curv, cross, square = [total[i * targets : (i + 1) * targets, :1] for i in range(4)]
    alpha = rz / curv
    direction = dir_ref[...]
    coef_out[...] = coef_ref[...] + alpha * direction
    resid = res_ref[...] - alpha * image_ref[...]
    res_out[...] = resid
    rz_new = rz - alpha * (2.0 * cross - alpha * square)
    dir_out[...] = pre_ref[...] * resid + (rz_new / rz) * direction


def small_call(kernel, outs, *args):
    return pl.pallas_call(
        kernel,
        out_shape=[jax.ShapeDtypeStruct(shape, F32) for shape in outs],
        in_specs=[VMEM] * len(args),
        out_specs=[VMEM] * len(outs),
        compiler_params=pltpu.CompilerParams(vmem_limit_bytes=8 * MIB),
    )(*args)


def shards(points, centres, coef, resid, direction, precond):
    num_pts, num_ctr = lax.axis_size("pts"), lax.axis_size("ctr")
    num, full = points.shape[1], direction.shape
    kern, part = fit_parts(points, centres, direction, 4)
    fits = over_ctr(part)
    (give_a,) = col_sums(fits, kern, (0,))
    got_a = send_pts(give_a, along(0))
    (keep_a,) = col_sums(fits, kern, (2,))
    (give_b,) = col_sums(fits, kern, (1,))
    got_b = send_pts(give_b, along(0))
    moved = send_pts(keep_a + got_a, along(1))
    (keep_b,) = col_sums(fits, kern, (3,))
    mine = moved + (keep_b + got_b)
    mine = sum_over_rest(mine)
    near = send_pts(mine, along(1))
    far = send_pts(mine, along(0))
    last = send_pts(near, along(0))
    scale = 2048.0 / (num * num_pts)
    pre = precond.reshape(1, full[1])
    image, sums = small_call(
        functools.partial(image_kernel, scale), [full, (4 * full[0], 128)], last, far, near, mine, direction, resid, pre
    )
    return small_call(
        functools.partial(step_kernel, num_ctr), [full] * 3, *over_ctr(sums), image, direction, resid, pre, coef
    )


def solution(mesh):
    return jax.shard_map(
        shards,
        mesh=mesh,
        in_specs=(
            P(None, "pts"),
            P(None, "ctr"),
            P(None, "ctr"),
            P(None, "ctr"),
            P(None, "ctr"),
            P("ctr"),
        ),
        out_specs=(P(None, "ctr"), P(None, "ctr"), P(None, "ctr")),
        check_vma=False,
    )
```

```python
import functools
import math

import jax
import jax.numpy as jnp
from jax import lax
from jax.experimental import pallas as pl
from jax.experimental.pallas import tpu as pltpu
from jax.sharding import PartitionSpec as P

MIB = 2**20
F32 = jnp.float32
BF16 = jnp.bfloat16
RATE = 0.25 * math.log2(math.e)
DEPTH = 128
VMEM = pl.BlockSpec(memory_space=pltpu.VMEM)


def tile_of(index, size):
    return pl.ds(pl.multiple_of(index * size, size), size)


def split3(value):
    first = value.astype(BF16).astype(F32)
    rest = value - first
    second = rest.astype(BF16).astype(F32)
    return first, second, rest - second


def rows_of(rows, block):
    at = lax.broadcasted_iota(jnp.int32, block, 0)
    out = jnp.zeros(block, F32)
    for i, row in enumerate(rows):
        out = jnp.where(at == i, row, out)
    return out


def fit_kernel(parts, width, pts_hbm, cen_hbm, dir_hbm, *refs):
    kern, (fit_ref, pts_ref, cen_ref, dir_ref, xa_ref, ca_ref, db_ref, sems) = refs[:parts], refs[parts:]
    pairs = ((pts_hbm, pts_ref), (cen_hbm, cen_ref), (dir_hbm, dir_ref))
    copies = [pltpu.make_async_copy(source, target, sems.at[i]) for i, (source, target) in enumerate(pairs)]
    for copy in copies:
        copy.start()
    feat, num = pts_ref.shape
    ctr = cen_ref.shape[1]
    copies[0].wait()
    pts = pts_ref[...].astype(F32)
    terms = list(split3(pts * RATE))
    norm = split3(jnp.sum(pts * pts, axis=0, keepdims=True) * (-0.5 * RATE))
    terms.append(rows_of(list(norm) + [1.0, 1.0, 1.0], (DEPTH - 3 * feat, num)))
    xa_ref[...] = jnp.concatenate(terms, axis=0).T.astype(BF16)
    copies[1].wait()
    cen = cen_ref[...]
    for i in range(3):
        ca_ref[i * feat : (i + 1) * feat, :] = cen
    cen = cen.astype(F32)
    norm = split3(jnp.sum(cen * cen, axis=0, keepdims=True) * (-0.5 * RATE))
    ca_ref[3 * feat :, :] = rows_of([1.0, 1.0, 1.0] + list(norm), (DEPTH - 3 * feat, ctr)).astype(BF16)
    copies[2].wait()
    db_ref[...] = dir_ref[...].astype(BF16)
    rows = num // parts

    def body(j, acc):
        col = tile_of(j, width)
        out = []
        for p in range(parts):
            logk = jnp.dot(xa_ref[p * rows : (p + 1) * rows, :], ca_ref[:, col], preferred_element_type=F32)
            tile = jnp.exp2(logk).astype(BF16)
            kern[p][:, col] = tile
            out.append(lax.dot_general(db_ref[:, col], tile, (((1,), (1,)), ((), ())), preferred_element_type=F32))
        return acc + jnp.concatenate(out, axis=1)

    acc = lax.fori_loop(0, ctr // width, body, jnp.zeros(fit_ref.shape, F32))
    fit_ref[...] = acc.astype(BF16)


def digits():
    me, odd = lax.axis_index("pts"), lax.axis_index("ctr") % 2
    low, high = me % 2, (me // 2) % 2
    return jnp.where(odd == 0, low, high), jnp.where(odd == 0, high, low)


def chunk_ids():
    a, b = digits()
    return 2 * (1 - a) + (1 - b), 2 * (1 - a) + b, 2 * a + (1 - b), 2 * a + b


def col_kernel(parts, groups, width, which, *refs):
    fits, kern, (out,) = refs[:groups], refs[groups : groups + parts], refs[groups + parts :]
    fitted = fits[0][...].astype(F32)
    for ref in fits[1:]:
        fitted = fitted + ref[...].astype(F32)
    fitted = fitted.astype(BF16)
    rows = kern[0].shape[0]
    steps = out.shape[1] // width
    first = chunk_ids()[which] * steps

    @pl.loop(0, steps)
    def _(j):
        col = tile_of(first + j, width)
        acc = None
        for p in range(parts):
            term = jnp.dot(fitted[:, p * rows : (p + 1) * rows], kern[p][:, col], preferred_element_type=F32)
            acc = term if acc is None else acc + term
        out[:, tile_of(j, width)] = acc


def width_of(size, most):
    width = most
    while size % width:
        width //= 2
    return width


def fit_parts(points, centres, direction, parts):
    num, ctr = points.shape[1], centres.shape[1]
    targets = direction.shape[0]
    out = pl.pallas_call(
        functools.partial(fit_kernel, parts, width_of(ctr, 1024)),
        out_shape=[jax.ShapeDtypeStruct((num // parts, ctr), BF16)] * parts + [jax.ShapeDtypeStruct((targets, num), BF16)],
        in_specs=[pl.BlockSpec(memory_space=pl.ANY)] * 3,
        out_specs=[VMEM] * (parts + 1),
        scratch_shapes=[
            pltpu.VMEM(points.shape, BF16),
            pltpu.VMEM(centres.shape, BF16),
            pltpu.VMEM(direction.shape, F32),
            pltpu.VMEM((num, DEPTH), BF16),
            pltpu.VMEM((DEPTH, ctr), BF16),
            pltpu.VMEM((targets, ctr), BF16),
            pltpu.SemaphoreType.DMA((3,)),
        ],
        compiler_params=pltpu.CompilerParams(vmem_limit_bytes=8 * MIB),
    )(*[pltpu.with_memory_space_constraint(value, pltpu.HBM) for value in (points, centres, direction)])
    return out[:parts], out[parts]


def col_sums(fits, kern, which):
    targets = fits[0].shape[0]
    size = kern[0].shape[1] // 4
    return pl.pallas_call(
        functools.partial(col_kernel, len(kern), len(fits), width_of(size, 2048), which),
        out_shape=jax.ShapeDtypeStruct((targets, size), F32),
        in_specs=[VMEM] * (len(fits) + len(kern)),
        out_specs=VMEM,
        compiler_params=pltpu.CompilerParams(vmem_limit_bytes=4 * MIB),
    )(*fits, *kern)


def radices(size):
    out, prime = [], 2
    while size > 1:
        while size % prime == 0:
            out.append(prime)
            size //= prime
        prime += 1
    return out


def send_pts(value, partner):
    num_pts, num_ctr = lax.axis_size("pts"), lax.axis_size("ctr")
    pairs = [(p * num_ctr + c, partner(p, c % 2) * num_ctr + c) for p in range(num_pts) for c in range(num_ctr)]
    return lax.ppermute(value, ("pts", "ctr"), pairs)


def along(phase):
    return lambda p, odd: p ^ (1 + (odd ^ phase))


def sum_over_rest(value):
    rest = lax.axis_size("pts") // 4
    twos = rest & -rest
    for k in range(twos.bit_length() - 1):
        mask = 4 * (2 * 2**k - 1)
        value = value + send_pts(value, lambda p, odd: p ^ mask)
    me, stride = lax.axis_index("pts"), 4 * twos
    for radix in radices(rest // twos):
        got = [value]
        for k in range(1, radix):

            def partner(p, odd):
                d = (p // stride) % radix
                return p + ((d + k) % radix - d) * stride

            got.append(send_pts(value, partner))
        mine, stack = (me // stride) % radix, jnp.stack(got)
        value = sum(lax.dynamic_index_in_dim(stack, (mine - d) % radix, 0, False) for d in range(radix))
        stride *= radix
    return value


def over_ctr(value):
    num_ctr = lax.axis_size("ctr")
    return [value] + [
        lax.ppermute(value, "ctr", [(c, (c + k) % num_ctr) for c in range(num_ctr)]) for k in range(1, num_ctr)
    ]


def image_kernel(scale, *refs):
    pieces, (dir_ref, res_ref, pre_ref, image_ref, sums_ref) = refs[:-5], refs[-5:]
    size = pieces[0].shape[1]
    each = len(pieces) // 4
    targets = sums_ref.shape[0] // 4
    sums = [jnp.zeros((targets, 1), F32)] * 4
    places = [chunk * each + i for chunk in chunk_ids() for i in range(each)]
    for piece, place in zip(pieces, places):
        col = tile_of(place, size)
        direction, resid, pre = dir_ref[:, col], res_ref[:, col], pre_ref[:, col]
        image = piece[...] * scale + 0.5 * direction
        image_ref[:, col] = image
        terms = (resid * resid * pre, direction * image, resid * pre * image, image * image * pre)
        sums = [old + jnp.sum(term, axis=1, keepdims=True) for old, term in zip(sums, terms)]
    for i, value in enumerate(sums):
        sums_ref[i * targets : (i + 1) * targets, :] = jnp.broadcast_to(value, (targets, 128))


def step_kernel(groups, *refs):
    image_ref, dir_ref, res_ref, pre_ref, coef_ref, coef_out, res_out, dir_out = refs[groups:]
    targets = dir_ref.shape[0]
    total = refs[0][...]
    for ref in refs[1:groups]:
        total = total + ref[...]
    rz, curv, cross, square = [total[i * targets : (i + 1) * targets, :1] for i in range(4)]
    alpha = rz / curv
    direction = dir_ref[...]
    coef_out[...] = coef_ref[...] + alpha * direction
    resid = res_ref[...] - alpha * image_ref[...]
    res_out[...] = resid
    rz_new = rz - alpha * (2.0 * cross - alpha * square)
    dir_out[...] = pre_ref[...] * resid + (rz_new / rz) * direction


def small_call(kernel, outs, *args):
    return pl.pallas_call(
        kernel,
        out_shape=[jax.ShapeDtypeStruct(shape, F32) for shape in outs],
        in_specs=[VMEM] * len(args),
        out_specs=[VMEM] * len(outs),
        compiler_params=pltpu.CompilerParams(vmem_limit_bytes=8 * MIB),
    )(*args)


def shards(points, centres, coef, resid, direction, precond):
    num_pts, num_ctr = lax.axis_size("pts"), lax.axis_size("ctr")
    num, full = points.shape[1], direction.shape
    kern, part = fit_parts(points, centres, direction, 4)
    fits = over_ctr(part)
    give_a = col_sums(fits, kern, 0)
    got_a = send_pts(give_a, along(0))
    keep_a = col_sums(fits, kern, 2)
    give_b = col_sums(fits, kern, 1)
    got_b = send_pts(give_b, along(0))
    moved = send_pts(keep_a + got_a, along(1))
    keep_b = col_sums(fits, kern, 3)
    mine = sum_over_rest(moved + (keep_b + got_b))
    near = send_pts(mine, along(1))
    far = send_pts(mine, along(0))
    last = send_pts(mine, lambda p, odd: p ^ 3)
    scale = 2048.0 / (num * num_pts)
    pre = precond.reshape(1, full[1])
    image, sums = small_call(
        functools.partial(image_kernel, scale), [full, (4 * full[0], 128)], last, far, near, mine, direction, resid, pre
    )
    return small_call(
        functools.partial(step_kernel, num_ctr), [full] * 3, *over_ctr(sums), image, direction, resid, pre, coef
    )


def solution(mesh):
    return jax.shard_map(
        shards,
        mesh=mesh,
        in_specs=(
            P(None, "pts"),
            P(None, "ctr"),
            P(None, "ctr"),
            P(None, "ctr"),
            P(None, "ctr"),
            P("ctr"),
        ),
        out_specs=(P(None, "ctr"), P(None, "ctr"), P(None, "ctr")),
        check_vma=False,
    )
```

```python
import functools
import math

import jax
import jax.numpy as jnp
from jax import lax
from jax.experimental import pallas as pl
from jax.experimental.pallas import tpu as pltpu
from jax.sharding import PartitionSpec as P

MIB = 2**20
F32 = jnp.float32
BF16 = jnp.bfloat16
RATE = 0.25 * math.log2(math.e)
DEPTH = 128
VMEM = pl.BlockSpec(memory_space=pltpu.VMEM)


def tile_of(index, size):
    return pl.ds(pl.multiple_of(index * size, size), size)


def split3(value):
    first = value.astype(BF16).astype(F32)
    rest = value - first
    second = rest.astype(BF16).astype(F32)
    return first, second, rest - second


def rows_of(rows, block):
    at = lax.broadcasted_iota(jnp.int32, block, 0)
    out = jnp.zeros(block, F32)
    for i, row in enumerate(rows):
        out = jnp.where(at == i, row, out)
    return out


def digits():
    me, odd = lax.axis_index("pts"), lax.axis_index("ctr") % 2
    low, high = me % 2, (me // 2) % 2
    return jnp.where(odd == 0, low, high), jnp.where(odd == 0, high, low)


def chunk_ids():
    a, b = digits()
    return 2 * (1 - a) + (1 - b), 2 * (1 - a) + b, 2 * a + (1 - b), 2 * a + b


def fit_kernel(width, across, pts_hbm, cen_hbm, dir_hbm, *refs):
    kern, (fit_ref, pts_ref, cen_ref, dir_ref, xa_ref, ca_ref, db_ref, sum_ref, sems) = refs[:4], refs[4:]
    pairs = ((pts_hbm, pts_ref), (cen_hbm, cen_ref), (dir_hbm, dir_ref))
    copies = [pltpu.make_async_copy(source, target, sems.at[i]) for i, (source, target) in enumerate(pairs)]
    for copy in copies:
        copy.start()
    feat, num = pts_ref.shape
    ctr = cen_ref.shape[1]
    copies[0].wait()
    pts = pts_ref[...].astype(F32)
    terms = list(split3(pts * RATE))
    norm = split3(jnp.sum(pts * pts, axis=0, keepdims=True) * (-0.5 * RATE))
    terms.append(rows_of(list(norm) + [1.0, 1.0, 1.0], (DEPTH - 3 * feat, num)))
    xa_ref[...] = jnp.concatenate(terms, axis=0).astype(BF16)
    copies[1].wait()
    cen = cen_ref[...]
    for i in range(3):
        ca_ref[i * feat : (i + 1) * feat, :] = cen
    cen = cen.astype(F32)
    norm = split3(jnp.sum(cen * cen, axis=0, keepdims=True) * (-0.5 * RATE))
    ca_ref[3 * feat :, :] = rows_of([1.0, 1.0, 1.0] + list(norm), (DEPTH - 3 * feat, ctr)).astype(BF16)
    copies[2].wait()
    db_ref[...] = dir_ref[...].astype(BF16)
    sum_ref[...] = jnp.zeros(sum_ref.shape, F32)
    steps = ctr // 4 // width
    for i, out in zip(chunk_ids(), kern):

        @pl.loop(0, steps)
        def _(j):
            col = tile_of(i * steps + j, width)
            cen = ca_ref[:, col].T
            for p in range(num // across):
                row = slice(p * across, (p + 1) * across)
                tile = jnp.exp2(jnp.dot(cen, xa_ref[:, row], preferred_element_type=F32)).astype(BF16)
                out[tile_of(j, width), row] = tile
                sum_ref[:, row] += jnp.dot(db_ref[:, col], tile, preferred_element_type=F32)

    fit_ref[...] = sum_ref[...].astype(BF16)


def col_kernel(width, *refs):
    fits, kern, out = refs[:-2], refs[-2], refs[-1]
    fitted = fits[0][...].astype(F32)
    for ref in fits[1:]:
        fitted = fitted + ref[...].astype(F32)
    fitted = fitted.astype(BF16)

    @pl.loop(0, out.shape[1] // width)
    def _(j):
        rows = tile_of(j, width)
        out[:, rows] = lax.dot_general(fitted, kern[rows, :], (((1,), (1,)), ((), ())), preferred_element_type=F32)


def width_of(size, most):
    width = most
    while size % width:
        width //= 2
    return width


def fit_parts(points, centres, direction):
    num, ctr = points.shape[1], centres.shape[1]
    targets = direction.shape[0]
    out = pl.pallas_call(
        functools.partial(fit_kernel, width_of(ctr // 4, 2048), width_of(num, 512)),
        out_shape=[jax.ShapeDtypeStruct((ctr // 4, num), BF16)] * 4 + [jax.ShapeDtypeStruct((targets, num), BF16)],
        in_specs=[pl.BlockSpec(memory_space=pl.ANY)] * 3,
        out_specs=[VMEM] * 5,
        scratch_shapes=[
            pltpu.VMEM(points.shape, BF16),
            pltpu.VMEM(centres.shape, BF16),
            pltpu.VMEM(direction.shape, F32),
            pltpu.VMEM((DEPTH, num), BF16),
            pltpu.VMEM((DEPTH, ctr), BF16),
            pltpu.VMEM((targets, ctr), BF16),
            pltpu.VMEM((targets, num), F32),
            pltpu.SemaphoreType.DMA((3,)),
        ],
        compiler_params=pltpu.CompilerParams(vmem_limit_bytes=18 * MIB),
    )(*[pltpu.with_memory_space_constraint(value, pltpu.HBM) for value in (points, centres, direction)])
    return out[:4], out[4]


def col_sums(fits, kern):
    targets = fits[0].shape[0]
    size = kern.shape[0]
    return pl.pallas_call(
        functools.partial(col_kernel, width_of(size, 2048)),
        out_shape=jax.ShapeDtypeStruct((targets, size), F32),
        in_specs=[VMEM] * (len(fits) + 1),
        out_specs=VMEM,
        compiler_params=pltpu.CompilerParams(vmem_limit_bytes=4 * MIB),
    )(*fits, kern)


def radices(size):
    out, prime = [], 2
    while size > 1:
        while size % prime == 0:
            out.append(prime)
            size //= prime
        prime += 1
    return out


def send_pts(value, partner):
    num_pts, num_ctr = lax.axis_size("pts"), lax.axis_size("ctr")
    pairs = [(p * num_ctr + c, partner(p, c % 2) * num_ctr + c) for p in range(num_pts) for c in range(num_ctr)]
    return lax.ppermute(value, ("pts", "ctr"), pairs)


def along(phase):
    return lambda p, odd: p ^ (1 + (odd ^ phase))


def sum_over_rest(value):
    rest = lax.axis_size("pts") // 4
    twos = rest & -rest
    for k in range(twos.bit_length() - 1):
        mask = 4 * (2 * 2**k - 1)
        value = value + send_pts(value, lambda p, odd: p ^ mask)
    me, stride = lax.axis_index("pts"), 4 * twos
    for radix in radices(rest // twos):
        got = [value]
        for k in range(1, radix):

            def partner(p, odd):
                d = (p // stride) % radix
                return p + ((d + k) % radix - d) * stride

            got.append(send_pts(value, partner))
        mine, stack = (me // stride) % radix, jnp.stack(got)
        value = sum(lax.dynamic_index_in_dim(stack, (mine - d) % radix, 0, False) for d in range(radix))
        stride *= radix
    return value


def over_ctr(value):
    num_ctr = lax.axis_size("ctr")
    return [value] + [
        lax.ppermute(value, "ctr", [(c, (c + k) % num_ctr) for c in range(num_ctr)]) for k in range(1, num_ctr)
    ]


def sums_kernel(scale, steps, *refs):
    chunks, others = refs[: len(steps)], refs[len(steps) : -4]
    dir_ref, res_ref, pre_ref, sums_ref = refs[-4:]
    size = chunks[0].shape[1]
    targets = sums_ref.shape[0] // 4
    sums = [other[i * targets : (i + 1) * targets, :1] for other in others for i in range(4)]
    sums = sums or [jnp.zeros((targets, 1), F32)] * 4
    ids = chunk_ids()
    for chunk, step in zip(chunks, steps):
        col = tile_of(ids[step], size)
        direction, resid, pre = dir_ref[:, col], res_ref[:, col], pre_ref[:, col]
        image = chunk[...] * scale + 0.5 * direction
        terms = (resid * resid * pre, direction * image, resid * pre * image, image * image * pre)
        sums = [old + jnp.sum(term, axis=1, keepdims=True) for old, term in zip(sums, terms)]
    for i, value in enumerate(sums):
        sums_ref[i * targets : (i + 1) * targets, :] = jnp.broadcast_to(value, (targets, 128))


def step_kernel(scale, groups, *refs):
    chunks, (dir_ref, res_ref, pre_ref, coef_ref) = refs[groups : groups + 4], refs[groups + 4 : groups + 8]
    coef_out, res_out, dir_out = refs[groups + 8 :]
    targets, size = chunks[0].shape
    total = refs[0][...]
    for ref in refs[1:groups]:
        total = total + ref[...]
    rz, curv, cross, square = [total[i * targets : (i + 1) * targets, :1] for i in range(4)]
    alpha = rz / curv
    beta = (rz - alpha * (2.0 * cross - alpha * square)) / rz
    for chunk, place in zip(chunks, chunk_ids()):
        col = tile_of(place, size)
        direction = dir_ref[:, col]
        coef_out[:, col] = coef_ref[:, col] + alpha * direction
        resid = res_ref[:, col] - alpha * (chunk[...] * scale + 0.5 * direction)
        res_out[:, col] = resid
        dir_out[:, col] = pre_ref[:, col] * resid + beta * direction


def sums_over(chunks, steps, others, scale, direction, resid, pre):
    args = [*chunks, *others, direction, resid, pre]
    return pl.pallas_call(
        functools.partial(sums_kernel, scale, steps),
        out_shape=jax.ShapeDtypeStruct((4 * direction.shape[0], 128), F32),
        in_specs=[VMEM] * len(args),
        out_specs=VMEM,
        compiler_params=pltpu.CompilerParams(vmem_limit_bytes=4 * MIB),
    )(*args)


def step_of(sums, chunks, scale, direction, resid, pre, coef):
    args = [*sums, *chunks, direction, resid, pre, coef]
    return pl.pallas_call(
        functools.partial(step_kernel, scale, len(sums)),
        out_shape=[jax.ShapeDtypeStruct(direction.shape, F32)] * 3,
        in_specs=[VMEM] * len(args),
        out_specs=[VMEM] * 3,
        compiler_params=pltpu.CompilerParams(vmem_limit_bytes=8 * MIB),
    )(*args)


def shards(points, centres, coef, resid, direction, precond):
    num_pts, num_ctr = lax.axis_size("pts"), lax.axis_size("ctr")
    num, full = points.shape[1], direction.shape
    kern, part = fit_parts(points, centres, direction)
    fits = over_ctr(part)
    give_a = col_sums(fits, kern[0])
    got_a = send_pts(give_a, along(0))
    keep_a = col_sums(fits, kern[2])
    give_b = col_sums(fits, kern[1])
    got_b = send_pts(give_b, along(0))
    moved = send_pts(keep_a + got_a, along(1))
    keep_b = col_sums(fits, kern[3])
    mine = sum_over_rest(moved + (keep_b + got_b))
    near = send_pts(mine, along(1))
    far = send_pts(mine, along(0))
    last = send_pts(mine, lambda p, odd: p ^ 3)
    scale = 2048.0 / (num * num_pts)
    pre = precond.reshape(1, full[1])
    rest = (scale, direction, resid, pre)
    early = sums_over([last, mine], (0, 3), [], *rest)
    sums = sums_over([far, near], (1, 2), [early], *rest)
    return step_of(over_ctr(sums), [last, far, near, mine], *rest, coef)


def solution(mesh):
    return jax.shard_map(
        shards,
        mesh=mesh,
        in_specs=(
            P(None, "pts"),
            P(None, "ctr"),
            P(None, "ctr"),
            P(None, "ctr"),
            P(None, "ctr"),
            P("ctr"),
        ),
        out_specs=(P(None, "ctr"), P(None, "ctr"), P(None, "ctr")),
        check_vma=False,
    )
```

```python
import functools
import math

import jax
import jax.numpy as jnp
from jax import lax
from jax.experimental import pallas as pl
from jax.experimental.pallas import tpu as pltpu
from jax.sharding import PartitionSpec as P

MIB = 2**20
F32 = jnp.float32
BF16 = jnp.bfloat16
RATE = 0.25 * math.log2(math.e)
DEPTH = 128
TURNED = (0, 2)
VMEM = pl.BlockSpec(memory_space=pltpu.VMEM)


def tile_of(index, size):
    return pl.ds(pl.multiple_of(index * size, size), size)


def split3(value):
    first = value.astype(BF16).astype(F32)
    rest = value - first
    second = rest.astype(BF16).astype(F32)
    return first, second, rest - second


def rows_of(rows, block):
    at = lax.broadcasted_iota(jnp.int32, block, 0)
    out = jnp.zeros(block, F32)
    for i, row in enumerate(rows):
        out = jnp.where(at == i, row, out)
    return out


def digits():
    me, odd = lax.axis_index("pts"), lax.axis_index("ctr") % 2
    low, high = me % 2, (me // 2) % 2
    return jnp.where(odd == 0, low, high), jnp.where(odd == 0, high, low)


def chunk_ids():
    a, b = digits()
    return 2 * (1 - a) + (1 - b), 2 * (1 - a) + b, 2 * a + (1 - b), 2 * a + b


def fit_kernel(width, across, pts_hbm, cen_hbm, dir_hbm, *refs):
    kern, (fit_ref, pts_ref, cen_ref, dir_ref, xa_ref, ca_ref, db_ref, sum_ref, sems) = refs[:4], refs[4:]
    pairs = ((pts_hbm, pts_ref), (cen_hbm, cen_ref), (dir_hbm, dir_ref))
    copies = [pltpu.make_async_copy(source, target, sems.at[i]) for i, (source, target) in enumerate(pairs)]
    for copy in copies:
        copy.start()
    feat, num = pts_ref.shape
    ctr = cen_ref.shape[1]
    copies[0].wait()
    pts = pts_ref[...].astype(F32)
    terms = list(split3(pts * RATE))
    norm = split3(jnp.sum(pts * pts, axis=0, keepdims=True) * (-0.5 * RATE))
    terms.append(rows_of(list(norm) + [1.0, 1.0, 1.0], (DEPTH - 3 * feat, num)))
    xa_ref[...] = jnp.concatenate(terms, axis=0).astype(BF16)
    copies[1].wait()
    cen = cen_ref[...]
    for i in range(3):
        ca_ref[i * feat : (i + 1) * feat, :] = cen
    cen = cen.astype(F32)
    norm = split3(jnp.sum(cen * cen, axis=0, keepdims=True) * (-0.5 * RATE))
    ca_ref[3 * feat :, :] = rows_of([1.0, 1.0, 1.0] + list(norm), (DEPTH - 3 * feat, ctr)).astype(BF16)
    copies[2].wait()
    db_ref[...] = dir_ref[...].astype(BF16)
    sum_ref[...] = jnp.zeros(sum_ref.shape, F32)
    steps = ctr // 4 // width
    for i, chunk, out in zip(range(4), chunk_ids(), kern):

        @pl.loop(0, steps)
        def _(j):
            col, place = tile_of(chunk * steps + j, width), tile_of(j, width)
            cen = ca_ref[:, col].T
            for p in range(num // across):
                row = slice(p * across, (p + 1) * across)
                tile = jnp.exp2(jnp.dot(cen, xa_ref[:, row], preferred_element_type=F32)).astype(BF16)
                if i in TURNED:
                    out[row, place] = tile.T
                else:
                    out[place, row] = tile
                sum_ref[:, row] += jnp.dot(db_ref[:, col], tile, preferred_element_type=F32)

    fit_ref[...] = sum_ref[...].astype(BF16)


def col_kernel(width, turned, *refs):
    fits, kern, out = refs[:-2], refs[-2], refs[-1]
    fitted = fits[0][...].astype(F32)
    for ref in fits[1:]:
        fitted = fitted + ref[...].astype(F32)
    fitted = fitted.astype(BF16)

    @pl.loop(0, out.shape[1] // width)
    def _(j):
        place = tile_of(j, width)
        tile = kern[:, place] if turned else kern[place, :]
        dims = (((1,), (0 if turned else 1,)), ((), ()))
        out[:, place] = lax.dot_general(fitted, tile, dims, preferred_element_type=F32)


def width_of(size, most):
    width = most
    while size % width:
        width //= 2
    return width


def fit_parts(points, centres, direction):
    num, ctr = points.shape[1], centres.shape[1]
    targets = direction.shape[0]
    shapes = [(num, ctr // 4) if i in TURNED else (ctr // 4, num) for i in range(4)] + [(targets, num)]
    out = pl.pallas_call(
        functools.partial(fit_kernel, width_of(ctr // 4, 2048), width_of(num, 512)),
        out_shape=[jax.ShapeDtypeStruct(shape, BF16) for shape in shapes],
        in_specs=[pl.BlockSpec(memory_space=pl.ANY)] * 3,
        out_specs=[VMEM] * 5,
        scratch_shapes=[
            pltpu.VMEM(points.shape, BF16),
            pltpu.VMEM(centres.shape, BF16),
            pltpu.VMEM(direction.shape, F32),
            pltpu.VMEM((DEPTH, num), BF16),
            pltpu.VMEM((DEPTH, ctr), BF16),
            pltpu.VMEM((targets, ctr), BF16),
            pltpu.VMEM((targets, num), F32),
            pltpu.SemaphoreType.DMA((3,)),
        ],
        compiler_params=pltpu.CompilerParams(vmem_limit_bytes=18 * MIB),
    )(*[pltpu.with_memory_space_constraint(value, pltpu.HBM) for value in (points, centres, direction)])
    return out[:4], out[4]


def col_sums(fits, kern, i):
    targets = fits[0].shape[0]
    size = kern[i].shape[1 if i in TURNED else 0]
    return pl.pallas_call(
        functools.partial(col_kernel, width_of(size, 2048), i in TURNED),
        out_shape=jax.ShapeDtypeStruct((targets, size), F32),
        in_specs=[VMEM] * (len(fits) + 1),
        out_specs=VMEM,
        compiler_params=pltpu.CompilerParams(vmem_limit_bytes=4 * MIB),
    )(*fits, kern[i])


def radices(size):
    out, prime = [], 2
    while size > 1:
        while size % prime == 0:
            out.append(prime)
            size //= prime
        prime += 1
    return out


def send_pts(value, partner):
    num_pts, num_ctr = lax.axis_size("pts"), lax.axis_size("ctr")
    pairs = [(p * num_ctr + c, partner(p, c % 2) * num_ctr + c) for p in range(num_pts) for c in range(num_ctr)]
    return lax.ppermute(value, ("pts", "ctr"), pairs)


def along(phase):
    return lambda p, odd: p ^ (1 + (odd ^ phase))


def sum_over_rest(value):
    rest = lax.axis_size("pts") // 4
    twos = rest & -rest
    for k in range(twos.bit_length() - 1):
        mask = 4 * (2 * 2**k - 1)
        value = value + send_pts(value, lambda p, odd: p ^ mask)
    me, stride = lax.axis_index("pts"), 4 * twos
    for radix in radices(rest // twos):
        got = [value]
        for k in range(1, radix):

            def partner(p, odd):
                d = (p // stride) % radix
                return p + ((d + k) % radix - d) * stride

            got.append(send_pts(value, partner))
        mine, stack = (me // stride) % radix, jnp.stack(got)
        value = sum(lax.dynamic_index_in_dim(stack, (mine - d) % radix, 0, False) for d in range(radix))
        stride *= radix
    return value


def over_ctr(value):
    num_ctr = lax.axis_size("ctr")
    return [value] + [
        lax.ppermute(value, "ctr", [(c, (c + k) % num_ctr) for c in range(num_ctr)]) for k in range(1, num_ctr)
    ]


def sums_kernel(scale, steps, *refs):
    chunks, others = refs[: len(steps)], refs[len(steps) : -4]
    dir_ref, res_ref, pre_ref, sums_ref = refs[-4:]
    size = chunks[0].shape[1]
    targets = sums_ref.shape[0] // 4
    sums = [other[i * targets : (i + 1) * targets, :1] for other in others for i in range(4)]
    sums = sums or [jnp.zeros((targets, 1), F32)] * 4
    ids = chunk_ids()
    for chunk, step in zip(chunks, steps):
        col = tile_of(ids[step], size)
        direction, resid, pre = dir_ref[:, col], res_ref[:, col], pre_ref[:, col]
        image = chunk[...] * scale + 0.5 * direction
        terms = (resid * resid * pre, direction * image, resid * pre * image, image * image * pre)
        sums = [old + jnp.sum(term, axis=1, keepdims=True) for old, term in zip(sums, terms)]
    for i, value in enumerate(sums):
        sums_ref[i * targets : (i + 1) * targets, :] = jnp.broadcast_to(value, (targets, 128))


def step_kernel(scale, groups, *refs):
    chunks, (dir_ref, res_ref, pre_ref, coef_ref) = refs[groups : groups + 4], refs[groups + 4 : groups + 8]
    coef_out, res_out, dir_out = refs[groups + 8 :]
    targets, size = chunks[0].shape
    total = refs[0][...]
    for ref in refs[1:groups]:
        total = total + ref[...]
    rz, curv, cross, square = [total[i * targets : (i + 1) * targets, :1] for i in range(4)]
    alpha = rz / curv
    beta = (rz - alpha * (2.0 * cross - alpha * square)) / rz
    for chunk, place in zip(chunks, chunk_ids()):
        col = tile_of(place, size)
        direction = dir_ref[:, col]
        coef_out[:, col] = coef_ref[:, col] + alpha * direction
        resid = res_ref[:, col] - alpha * (chunk[...] * scale + 0.5 * direction)
        res_out[:, col] = resid
        dir_out[:, col] = pre_ref[:, col] * resid + beta * direction


def sums_over(chunks, steps, others, scale, direction, resid, pre):
    args = [*chunks, *others, direction, resid, pre]
    return pl.pallas_call(
        functools.partial(sums_kernel, scale, steps),
        out_shape=jax.ShapeDtypeStruct((4 * direction.shape[0], 128), F32),
        in_specs=[VMEM] * len(args),
        out_specs=VMEM,
        compiler_params=pltpu.CompilerParams(vmem_limit_bytes=4 * MIB),
    )(*args)


def step_of(sums, chunks, scale, direction, resid, pre, coef):
    args = [*sums, *chunks, direction, resid, pre, coef]
    return pl.pallas_call(
        functools.partial(step_kernel, scale, len(sums)),
        out_shape=[jax.ShapeDtypeStruct(direction.shape, F32)] * 3,
        in_specs=[VMEM] * len(args),
        out_specs=[VMEM] * 3,
        compiler_params=pltpu.CompilerParams(vmem_limit_bytes=8 * MIB),
    )(*args)


def shards(points, centres, coef, resid, direction, precond):
    num_pts, num_ctr = lax.axis_size("pts"), lax.axis_size("ctr")
    num, full = points.shape[1], direction.shape
    kern, part = fit_parts(points, centres, direction)
    fits = over_ctr(part)
    give_a = col_sums(fits, kern, 0)
    got_a = send_pts(give_a, along(0))
    keep_a = col_sums(fits, kern, 2)
    give_b = col_sums(fits, kern, 1)
    got_b = send_pts(give_b, along(0))
    moved = send_pts(keep_a + got_a, along(1))
    keep_b = col_sums(fits, kern, 3)
    mine = sum_over_rest(moved + (keep_b + got_b))
    near = send_pts(mine, along(1))
    far = send_pts(mine, along(0))
    last = send_pts(mine, lambda p, odd: p ^ 3)
    scale = 2048.0 / (num * num_pts)
    pre = precond.reshape(1, full[1])
    rest = (scale, direction, resid, pre)
    early = sums_over([last, mine], (0, 3), [], *rest)
    sums = sums_over([far, near], (1, 2), [early], *rest)
    return step_of(over_ctr(sums), [last, far, near, mine], *rest, coef)


def solution(mesh):
    return jax.shard_map(
        shards,
        mesh=mesh,
        in_specs=(
            P(None, "pts"),
            P(None, "ctr"),
            P(None, "ctr"),
            P(None, "ctr"),
            P(None, "ctr"),
            P("ctr"),
        ),
        out_specs=(P(None, "ctr"), P(None, "ctr"), P(None, "ctr")),
        check_vma=False,
    )
```

```python
import functools
import math

import jax
import jax.numpy as jnp
from jax import lax
from jax.experimental import pallas as pl
from jax.experimental.pallas import tpu as pltpu
from jax.sharding import PartitionSpec as P

MIB = 2**20
F32 = jnp.float32
BF16 = jnp.bfloat16
RATE = 0.25 * math.log2(math.e)
DEPTH = 128
TURNED = (0, 1, 2)
VMEM = pl.BlockSpec(memory_space=pltpu.VMEM)


def tile_of(index, size):
    return pl.ds(pl.multiple_of(index * size, size), size)


def split3(value):
    first = value.astype(BF16).astype(F32)
    rest = value - first
    second = rest.astype(BF16).astype(F32)
    return first, second, rest - second


def rows_of(rows, block):
    at = lax.broadcasted_iota(jnp.int32, block, 0)
    out = jnp.zeros(block, F32)
    for i, row in enumerate(rows):
        out = jnp.where(at == i, row, out)
    return out


def digits():
    me, odd = lax.axis_index("pts"), lax.axis_index("ctr") % 2
    low, high = me % 2, (me // 2) % 2
    return jnp.where(odd == 0, low, high), jnp.where(odd == 0, high, low)


def chunk_ids():
    a, b = digits()
    return 2 * (1 - a) + (1 - b), 2 * (1 - a) + b, 2 * a + (1 - b), 2 * a + b


def fit_kernel(width, across, pts_hbm, cen_hbm, dir_hbm, *refs):
    kern, (fit_ref, pts_ref, cen_ref, dir_ref, xa_ref, sum_ref, sems) = refs[:4], refs[4:11]
    ca_refs, db_refs = refs[11:15], refs[15:]
    pairs = ((pts_hbm, pts_ref), (cen_hbm, cen_ref), (dir_hbm, dir_ref))
    copies = [pltpu.make_async_copy(source, target, sems.at[i]) for i, (source, target) in enumerate(pairs)]
    for copy in copies:
        copy.start()
    feat, num = pts_ref.shape
    ctr = cen_ref.shape[1]
    copies[0].wait()
    pts = pts_ref[...].astype(F32)
    terms = list(split3(pts * RATE))
    norm = split3(jnp.sum(pts * pts, axis=0, keepdims=True) * (-0.5 * RATE))
    terms.append(rows_of(list(norm) + [1.0, 1.0, 1.0], (DEPTH - 3 * feat, num)))
    xa_ref[...] = jnp.concatenate(terms, axis=0).astype(BF16)
    size = ctr // 4
    ids = chunk_ids()

    def features(i):
        col = tile_of(ids[i], size)
        cen = cen_ref[:, col]
        wide = cen.astype(F32)
        norm = split3(jnp.sum(wide * wide, axis=0, keepdims=True) * (-0.5 * RATE))
        block = rows_of([1.0, 1.0, 1.0] + list(norm), (DEPTH - 3 * feat, size)).astype(BF16)
        ca_refs[i][...] = jnp.concatenate([cen, cen, cen, block], axis=0).T
        db_refs[i][...] = dir_ref[:, col].astype(BF16)

    copies[1].wait()
    copies[2].wait()
    features(0)
    sum_ref[...] = jnp.zeros(sum_ref.shape, F32)
    waiting = []
    for i, out in enumerate(kern):
        for p in range(num // across):
            row = slice(p * across, (p + 1) * across)
            for j in range(size // width):
                place = slice(j * width, (j + 1) * width)
                tile = jnp.exp2(jnp.dot(ca_refs[i][place, :], xa_ref[:, row], preferred_element_type=F32)).astype(BF16)
                if i in TURNED:
                    out[row, place] = tile.T
                else:
                    out[place, row] = tile
                waiting.append((i, row, place, tile))
                if len(waiting) > 2:
                    k, old_row, old_place, old = waiting.pop(0)
                    sum_ref[:, old_row] += jnp.dot(db_refs[k][:, old_place], old, preferred_element_type=F32)
            if i < 3 and p == 0:
                features(i + 1)

    for k, old_row, old_place, old in waiting:
        sum_ref[:, old_row] += jnp.dot(db_refs[k][:, old_place], old, preferred_element_type=F32)
    fit_ref[...] = sum_ref[...].astype(BF16)


def col_kernel(width, turned, *refs):
    fits, kern, out = refs[:-2], refs[-2], refs[-1]
    fitted = fits[0][...].astype(F32)
    for ref in fits[1:]:
        fitted = fitted + ref[...].astype(F32)
    fitted = fitted.astype(BF16)

    @pl.loop(0, out.shape[1] // width)
    def _(j):
        place = tile_of(j, width)
        tile = kern[:, place] if turned else kern[place, :]
        dims = (((1,), (0 if turned else 1,)), ((), ()))
        out[:, place] = lax.dot_general(fitted, tile, dims, preferred_element_type=F32)


def width_of(size, most):
    width = most
    while size % width:
        width //= 2
    return width


def fit_parts(points, centres, direction):
    num, ctr = points.shape[1], centres.shape[1]
    targets = direction.shape[0]
    shapes = [(num, ctr // 4) if i in TURNED else (ctr // 4, num) for i in range(4)] + [(targets, num)]
    out = pl.pallas_call(
        functools.partial(fit_kernel, width_of(ctr // 4, 2048), width_of(num, 256)),
        out_shape=[jax.ShapeDtypeStruct(shape, BF16) for shape in shapes],
        in_specs=[pl.BlockSpec(memory_space=pl.ANY)] * 3,
        out_specs=[VMEM] * 5,
        scratch_shapes=[
            pltpu.VMEM(points.shape, BF16),
            pltpu.VMEM(centres.shape, BF16),
            pltpu.VMEM(direction.shape, F32),
            pltpu.VMEM((DEPTH, num), BF16),
            pltpu.VMEM((targets, num), F32),
            pltpu.SemaphoreType.DMA((3,)),
        ]
        + [pltpu.VMEM((ctr // 4, DEPTH), BF16)] * 4
        + [pltpu.VMEM((targets, ctr // 4), BF16)] * 4,
        compiler_params=pltpu.CompilerParams(vmem_limit_bytes=18 * MIB),
    )(*[pltpu.with_memory_space_constraint(value, pltpu.HBM) for value in (points, centres, direction)])
    return out[:4], out[4]


def col_sums(fits, kern, i):
    targets = fits[0].shape[0]
    size = kern[i].shape[1 if i in TURNED else 0]
    return pl.pallas_call(
        functools.partial(col_kernel, width_of(size, 2048), i in TURNED),
        out_shape=jax.ShapeDtypeStruct((targets, size), F32),
        in_specs=[VMEM] * (len(fits) + 1),
        out_specs=VMEM,
        compiler_params=pltpu.CompilerParams(vmem_limit_bytes=4 * MIB),
    )(*fits, kern[i])


def radices(size):
    out, prime = [], 2
    while size > 1:
        while size % prime == 0:
            out.append(prime)
            size //= prime
        prime += 1
    return out


def send_pts(value, partner):
    num_pts, num_ctr = lax.axis_size("pts"), lax.axis_size("ctr")
    pairs = [(p * num_ctr + c, partner(p, c % 2) * num_ctr + c) for p in range(num_pts) for c in range(num_ctr)]
    return lax.ppermute(value, ("pts", "ctr"), pairs)


def along(phase):
    return lambda p, odd: p ^ (1 + (odd ^ phase))


def sum_over_rest(value):
    rest = lax.axis_size("pts") // 4
    twos = rest & -rest
    for k in range(twos.bit_length() - 1):
        mask = 4 * (2 * 2**k - 1)
        value = value + send_pts(value, lambda p, odd: p ^ mask)
    me, stride = lax.axis_index("pts"), 4 * twos
    for radix in radices(rest // twos):
        got = [value]
        for k in range(1, radix):

            def partner(p, odd):
                d = (p // stride) % radix
                return p + ((d + k) % radix - d) * stride

            got.append(send_pts(value, partner))
        mine, stack = (me // stride) % radix, jnp.stack(got)
        value = sum(lax.dynamic_index_in_dim(stack, (mine - d) % radix, 0, False) for d in range(radix))
        stride *= radix
    return value


def over_ctr(value):
    num_ctr = lax.axis_size("ctr")
    return [value] + [
        lax.ppermute(value, "ctr", [(c, (c + k) % num_ctr) for c in range(num_ctr)]) for k in range(1, num_ctr)
    ]


def sums_kernel(scale, steps, *refs):
    chunks, others = refs[: len(steps)], refs[len(steps) : -4]
    dir_ref, res_ref, pre_ref, sums_ref = refs[-4:]
    size = chunks[0].shape[1]
    targets = sums_ref.shape[0] // 4
    sums = [other[i * targets : (i + 1) * targets, :1] for other in others for i in range(4)]
    sums = sums or [jnp.zeros((targets, 1), F32)] * 4
    ids = chunk_ids()
    for chunk, step in zip(chunks, steps):
        col = tile_of(ids[step], size)
        direction, resid, pre = dir_ref[:, col], res_ref[:, col], pre_ref[:, col]
        image = chunk[...] * scale + 0.5 * direction
        terms = (resid * resid * pre, direction * image, resid * pre * image, image * image * pre)
        sums = [old + jnp.sum(term, axis=1, keepdims=True) for old, term in zip(sums, terms)]
    for i, value in enumerate(sums):
        sums_ref[i * targets : (i + 1) * targets, :] = jnp.broadcast_to(value, (targets, 128))


def step_kernel(scale, groups, *refs):
    chunks, (dir_ref, res_ref, pre_ref, coef_ref) = refs[groups : groups + 4], refs[groups + 4 : groups + 8]
    coef_out, res_out, dir_out = refs[groups + 8 :]
    targets, size = chunks[0].shape
    total = refs[0][...]
    for ref in refs[1:groups]:
        total = total + ref[...]
    rz, curv, cross, square = [total[i * targets : (i + 1) * targets, :1] for i in range(4)]
    alpha = rz / curv
    beta = (rz - alpha * (2.0 * cross - alpha * square)) / rz
    for chunk, place in zip(chunks, chunk_ids()):
        col = tile_of(place, size)
        direction = dir_ref[:, col]
        coef_out[:, col] = coef_ref[:, col] + alpha * direction
        resid = res_ref[:, col] - alpha * (chunk[...] * scale + 0.5 * direction)
        res_out[:, col] = resid
        dir_out[:, col] = pre_ref[:, col] * resid + beta * direction


def sums_over(chunks, steps, others, scale, direction, resid, pre):
    args = [*chunks, *others, direction, resid, pre]
    return pl.pallas_call(
        functools.partial(sums_kernel, scale, steps),
        out_shape=jax.ShapeDtypeStruct((4 * direction.shape[0], 128), F32),
        in_specs=[VMEM] * len(args),
        out_specs=VMEM,
        compiler_params=pltpu.CompilerParams(vmem_limit_bytes=4 * MIB),
    )(*args)


def step_of(sums, chunks, scale, direction, resid, pre, coef):
    args = [*sums, *chunks, direction, resid, pre, coef]
    return pl.pallas_call(
        functools.partial(step_kernel, scale, len(sums)),
        out_shape=[jax.ShapeDtypeStruct(direction.shape, F32)] * 3,
        in_specs=[VMEM] * len(args),
        out_specs=[VMEM] * 3,
        compiler_params=pltpu.CompilerParams(vmem_limit_bytes=8 * MIB),
    )(*args)


def shards(points, centres, coef, resid, direction, precond):
    num_pts, num_ctr = lax.axis_size("pts"), lax.axis_size("ctr")
    num, full = points.shape[1], direction.shape
    kern, part = fit_parts(points, centres, direction)
    fits = over_ctr(part)
    give_a = col_sums(fits, kern, 0)
    got_a = send_pts(give_a, along(0))
    keep_a = col_sums(fits, kern, 2)
    give_b = col_sums(fits, kern, 1)
    got_b = send_pts(give_b, along(0))
    moved = send_pts(keep_a + got_a, along(1))
    keep_b = col_sums(fits, kern, 3)
    mine = sum_over_rest(moved + (keep_b + got_b))
    near = send_pts(mine, along(1))
    far = send_pts(mine, along(0))
    last = send_pts(mine, lambda p, odd: p ^ 3)
    scale = 2048.0 / (num * num_pts)
    pre = precond.reshape(1, full[1])
    rest = (scale, direction, resid, pre)
    early = sums_over([last, mine], (0, 3), [], *rest)
    sums = sums_over([far, near], (1, 2), [early], *rest)
    return step_of(over_ctr(sums), [last, far, near, mine], *rest, coef)


def solution(mesh):
    return jax.shard_map(
        shards,
        mesh=mesh,
        in_specs=(
            P(None, "pts"),
            P(None, "ctr"),
            P(None, "ctr"),
            P(None, "ctr"),
            P(None, "ctr"),
            P("ctr"),
        ),
        out_specs=(P(None, "ctr"), P(None, "ctr"), P(None, "ctr")),
        check_vma=False,
    )
```

```python
import functools
import math

import jax
import jax.numpy as jnp
from jax import lax
from jax.experimental import pallas as pl
from jax.experimental.pallas import tpu as pltpu
from jax.sharding import PartitionSpec as P

MIB = 2**20
F32 = jnp.float32
BF16 = jnp.bfloat16
RATE = 0.25 * math.log2(math.e)
DEPTH = 128
TURNED = (0, 1, 2)
VMEM = pl.BlockSpec(memory_space=pltpu.VMEM)


def tile_of(index, size):
    return pl.ds(pl.multiple_of(index * size, size), size)


def split3(value):
    first = value.astype(BF16).astype(F32)
    rest = value - first
    second = rest.astype(BF16).astype(F32)
    return first, second, rest - second


def rows_of(rows, block):
    at = lax.broadcasted_iota(jnp.int32, block, 0)
    out = jnp.zeros(block, F32)
    for i, row in enumerate(rows):
        out = jnp.where(at == i, row, out)
    return out


def digits():
    me, odd = lax.axis_index("pts"), lax.axis_index("ctr") % 2
    low, high = me % 2, (me // 2) % 2
    return jnp.where(odd == 0, low, high), jnp.where(odd == 0, high, low)


def chunk_ids():
    a, b = digits()
    return 2 * (1 - a) + (1 - b), 2 * (1 - a) + b, 2 * a + (1 - b), 2 * a + b


def fit_kernel(width, across, pts_hbm, cen_hbm, dir_hbm, *refs):
    kern, (fit_ref, pts_ref, cen_ref, dir_ref, xa_ref, sum_ref, sems) = refs[:4], refs[4:11]
    ca_refs, db_refs = refs[11:15], refs[15:]
    pairs = ((pts_hbm, pts_ref), (cen_hbm, cen_ref), (dir_hbm, dir_ref))
    copies = [pltpu.make_async_copy(source, target, sems.at[i]) for i, (source, target) in enumerate(pairs)]
    for copy in copies:
        copy.start()
    feat, num = pts_ref.shape
    ctr = cen_ref.shape[1]
    copies[0].wait()
    pts = pts_ref[...].astype(F32)
    terms = list(split3(pts * RATE))
    norm = split3(jnp.sum(pts * pts, axis=0, keepdims=True) * (-0.5 * RATE))
    terms.append(rows_of(list(norm) + [1.0, 1.0, 1.0], (DEPTH - 3 * feat, num)))
    xa_ref[...] = jnp.concatenate(terms, axis=0).astype(BF16)
    size = ctr // 4
    ids = chunk_ids()

    def features(i):
        col = tile_of(ids[i], size)
        cen = cen_ref[:, col]
        wide = cen.astype(F32)
        norm = split3(jnp.sum(wide * wide, axis=0, keepdims=True) * (-0.5 * RATE))
        block = rows_of([1.0, 1.0, 1.0] + list(norm), (DEPTH - 3 * feat, size)).astype(BF16)
        ca_refs[i][...] = jnp.concatenate([cen, cen, cen, block], axis=0).T
        db_refs[i][...] = dir_ref[:, col].astype(BF16)

    copies[1].wait()
    copies[2].wait()
    features(0)
    sum_ref[...] = jnp.zeros(sum_ref.shape, F32)
    waiting = []
    for i, out in enumerate(kern):
        for p in range(num // across):
            row = slice(p * across, (p + 1) * across)
            for j in range(size // width):
                place = slice(j * width, (j + 1) * width)
                tile = jnp.exp2(jnp.dot(ca_refs[i][place, :], xa_ref[:, row], preferred_element_type=F32)).astype(BF16)
                if i in TURNED:
                    out[row, place] = tile.T
                else:
                    out[place, row] = tile
                waiting.append((i, row, place, tile))
                if len(waiting) > 1:
                    k, old_row, old_place, old = waiting.pop(0)
                    sum_ref[:, old_row] += jnp.dot(db_refs[k][:, old_place], old, preferred_element_type=F32)
            if i < 3 and p == 0:
                features(i + 1)

    for k, old_row, old_place, old in waiting:
        sum_ref[:, old_row] += jnp.dot(db_refs[k][:, old_place], old, preferred_element_type=F32)
    fit_ref[...] = sum_ref[...].astype(BF16)


def col_kernel(width, turned, *refs):
    fits, kern, out = refs[:-2], refs[-2], refs[-1]
    fitted = fits[0][...].astype(F32)
    for ref in fits[1:]:
        fitted = fitted + ref[...].astype(F32)
    fitted = fitted.astype(BF16)

    @pl.loop(0, out.shape[1] // width)
    def _(j):
        place = tile_of(j, width)
        tile = kern[:, place] if turned else kern[place, :]
        dims = (((1,), (0 if turned else 1,)), ((), ()))
        out[:, place] = lax.dot_general(fitted, tile, dims, preferred_element_type=F32)


def width_of(size, most):
    width = most
    while size % width:
        width //= 2
    return width


def fit_parts(points, centres, direction):
    num, ctr = points.shape[1], centres.shape[1]
    targets = direction.shape[0]
    shapes = [(num, ctr // 4) if i in TURNED else (ctr // 4, num) for i in range(4)] + [(targets, num)]
    out = pl.pallas_call(
        functools.partial(fit_kernel, width_of(ctr // 4, 2048), width_of(num, 256)),
        out_shape=[jax.ShapeDtypeStruct(shape, BF16) for shape in shapes],
        in_specs=[pl.BlockSpec(memory_space=pl.ANY)] * 3,
        out_specs=[VMEM] * 5,
        scratch_shapes=[
            pltpu.VMEM(points.shape, BF16),
            pltpu.VMEM(centres.shape, BF16),
            pltpu.VMEM(direction.shape, F32),
            pltpu.VMEM((DEPTH, num), BF16),
            pltpu.VMEM((targets, num), F32),
            pltpu.SemaphoreType.DMA((3,)),
        ]
        + [pltpu.VMEM((ctr // 4, DEPTH), BF16)] * 4
        + [pltpu.VMEM((targets, ctr // 4), BF16)] * 4,
        compiler_params=pltpu.CompilerParams(vmem_limit_bytes=12 * MIB),
    )(*[pltpu.with_memory_space_constraint(value, pltpu.HBM) for value in (points, centres, direction)])
    return out[:4], out[4]


def col_sums(fits, kern, i):
    targets = fits[0].shape[0]
    size = kern[i].shape[1 if i in TURNED else 0]
    return pl.pallas_call(
        functools.partial(col_kernel, width_of(size, 2048), i in TURNED),
        out_shape=jax.ShapeDtypeStruct((targets, size), F32),
        in_specs=[VMEM] * (len(fits) + 1),
        out_specs=VMEM,
        compiler_params=pltpu.CompilerParams(vmem_limit_bytes=4 * MIB),
    )(*fits, kern[i])


def radices(size):
    out, prime = [], 2
    while size > 1:
        while size % prime == 0:
            out.append(prime)
            size //= prime
        prime += 1
    return out


def send_pts(value, partner):
    num_pts, num_ctr = lax.axis_size("pts"), lax.axis_size("ctr")
    pairs = [(p * num_ctr + c, partner(p, c % 2) * num_ctr + c) for p in range(num_pts) for c in range(num_ctr)]
    return lax.ppermute(value, ("pts", "ctr"), pairs)


def along(phase):
    return lambda p, odd: p ^ (1 + (odd ^ phase))


def sum_over_rest(value):
    rest = lax.axis_size("pts") // 4
    twos = rest & -rest
    for k in range(twos.bit_length() - 1):
        mask = 4 * (2 * 2**k - 1)
        value = value + send_pts(value, lambda p, odd: p ^ mask)
    me, stride = lax.axis_index("pts"), 4 * twos
    for radix in radices(rest // twos):
        got = [value]
        for k in range(1, radix):

            def partner(p, odd):
                d = (p // stride) % radix
                return p + ((d + k) % radix - d) * stride

            got.append(send_pts(value, partner))
        mine, stack = (me // stride) % radix, jnp.stack(got)
        value = sum(lax.dynamic_index_in_dim(stack, (mine - d) % radix, 0, False) for d in range(radix))
        stride *= radix
    return value


def over_ctr(value):
    num_ctr = lax.axis_size("ctr")
    return [value] + [
        lax.ppermute(value, "ctr", [(c, (c + k) % num_ctr) for c in range(num_ctr)]) for k in range(1, num_ctr)
    ]


def sums_kernel(scale, steps, *refs):
    chunks, others = refs[: len(steps)], refs[len(steps) : -4]
    dir_ref, res_ref, pre_ref, sums_ref = refs[-4:]
    size = chunks[0].shape[1]
    targets = sums_ref.shape[0] // 4
    sums = [other[i * targets : (i + 1) * targets, :1] for other in others for i in range(4)]
    sums = sums or [jnp.zeros((targets, 1), F32)] * 4
    ids = chunk_ids()
    for chunk, step in zip(chunks, steps):
        col = tile_of(ids[step], size)
        direction, resid, pre = dir_ref[:, col], res_ref[:, col], pre_ref[:, col]
        image = chunk[...] * scale + 0.5 * direction
        terms = (resid * resid * pre, direction * image, resid * pre * image, image * image * pre)
        sums = [old + jnp.sum(term, axis=1, keepdims=True) for old, term in zip(sums, terms)]
    for i, value in enumerate(sums):
        sums_ref[i * targets : (i + 1) * targets, :] = jnp.broadcast_to(value, (targets, 128))


def step_kernel(scale, groups, *refs):
    chunks, (dir_ref, res_ref, pre_ref, coef_ref) = refs[groups : groups + 4], refs[groups + 4 : groups + 8]
    coef_out, res_out, dir_out = refs[groups + 8 :]
    targets, size = chunks[0].shape
    total = refs[0][...]
    for ref in refs[1:groups]:
        total = total + ref[...]
    rz, curv, cross, square = [total[i * targets : (i + 1) * targets, :1] for i in range(4)]
    alpha = rz / curv
    beta = (rz - alpha * (2.0 * cross - alpha * square)) / rz
    for chunk, place in zip(chunks, chunk_ids()):
        col = tile_of(place, size)
        direction = dir_ref[:, col]
        coef_out[:, col] = coef_ref[:, col] + alpha * direction
        resid = res_ref[:, col] - alpha * (chunk[...] * scale + 0.5 * direction)
        res_out[:, col] = resid
        dir_out[:, col] = pre_ref[:, col] * resid + beta * direction


def sums_over(chunks, steps, others, scale, direction, resid, pre):
    args = [*chunks, *others, direction, resid, pre]
    return pl.pallas_call(
        functools.partial(sums_kernel, scale, steps),
        out_shape=jax.ShapeDtypeStruct((4 * direction.shape[0], 128), F32),
        in_specs=[VMEM] * len(args),
        out_specs=VMEM,
        compiler_params=pltpu.CompilerParams(vmem_limit_bytes=4 * MIB),
    )(*args)


def step_of(sums, chunks, scale, direction, resid, pre, coef):
    args = [*sums, *chunks, direction, resid, pre, coef]
    return pl.pallas_call(
        functools.partial(step_kernel, scale, len(sums)),
        out_shape=[jax.ShapeDtypeStruct(direction.shape, F32)] * 3,
        in_specs=[VMEM] * len(args),
        out_specs=[VMEM] * 3,
        compiler_params=pltpu.CompilerParams(vmem_limit_bytes=8 * MIB),
    )(*args)


def shards(points, centres, coef, resid, direction, precond):
    num_pts, num_ctr = lax.axis_size("pts"), lax.axis_size("ctr")
    num, full = points.shape[1], direction.shape
    kern, part = fit_parts(points, centres, direction)
    fits = over_ctr(part)
    give_a = col_sums(fits, kern, 0)
    got_a = send_pts(give_a, along(0))
    keep_a = col_sums(fits, kern, 2)
    give_b = col_sums(fits, kern, 1)
    got_b = send_pts(give_b, along(0))
    moved = send_pts(keep_a + got_a, along(1))
    keep_b = col_sums(fits, kern, 3)
    mine = sum_over_rest(moved + (keep_b + got_b))
    near = send_pts(mine, along(1))
    far = send_pts(mine, along(0))
    last = send_pts(mine, lambda p, odd: p ^ 3)
    scale = 2048.0 / (num * num_pts)
    pre = precond.reshape(1, full[1])
    rest = (scale, direction, resid, pre)
    early = sums_over([last, mine], (0, 3), [], *rest)
    sums = sums_over([far, near], (1, 2), [early], *rest)
    return step_of(over_ctr(sums), [last, far, near, mine], *rest, coef)


def solution(mesh):
    return jax.shard_map(
        shards,
        mesh=mesh,
        in_specs=(
            P(None, "pts"),
            P(None, "ctr"),
            P(None, "ctr"),
            P(None, "ctr"),
            P(None, "ctr"),
            P("ctr"),
        ),
        out_specs=(P(None, "ctr"), P(None, "ctr"), P(None, "ctr")),
        check_vma=False,
    )
```
